32 devices in a mesh: parts: 2 (over x), lat: 16 (over z, y, core).
Axes of the slice: x: 2, y: 2, z: 4, core: 2. Of those that a mesh axis runs over, the one named last changes fastest.
Arguments:
- state: float32 [64, 512, 128], P(('parts', 'lat')), parts along dimension 0, may hold values from -6 to 6
- east_wind: float32 [64, 512, 128], P(('parts', 'lat')), parts along dimension 0, may hold values from -6 to 6
- north_wind: float32 [64, 512, 128], P(('parts', 'lat')), parts along dimension 0, may hold values from -6 to 6
- coef: float32 [64, 512], P('parts'), parts along dimension 0, may hold values from 0.5 to 2
- project: float32 [128, 128], replicated, may hold values from -0.5 to 0.5
- restore: float32 [128, 128], replicated, may hold values from -0.5 to 0.5
- stiffness: float32 [128], replicated, may hold values from 4 to 1000
- sweeps: int32 [128], replicated, may hold values from 2 to 8
- mode_slots: int32 [32, 2], P('parts'), parts along dimension 0, may hold values from -1 to 127, as said below
Outputs:
- next_state: float32 [64, 512, 128], P(('parts', 'lat')), parts along dimension 0
The draws below stay inside these ranges and needn't reach their ends.
There are 2 independent parts, one for each index of `parts`. The reference program is written for one: setup_inputs(seed, part) draws one part's arguments, and reference() takes and returns one part's arrays. A program takes and returns all parts, laid end to end along the dimension named above; an argument that names none is the same for every part. Nothing has to cross between parts.
Inputs may be any that keep to these rules, and one draw needn't show every extreme that they name: `mode_slots`: row i lists the modes that device i of lat solves, -1 for an empty slot; exactly 12 distinct modes are listed in all, and some row is full.
All inputs are finite; a program needn't handle non-finite values.
Results may differ from the reference program's by a relative error of at most 0.00005.
Values sent between devices are 32-bit elements; how exact they have to be, the bound alone decides.
A program may use at most 64 MiB of HBM per device.

```python
import math
import jax
import jax.numpy as jnp
from jax import lax

K = 128
NLON = 512
SLOTS = 2
OWNERS = 16
NLAT = 32
IMPL = 12


def draw_mode_slots(key, part):
    first, second, third = jax.random.split(key, 3)
    chosen = jax.random.permutation(first, K)[:IMPL].astype(jnp.int32)
    total = OWNERS * SLOTS
    ranking = jax.random.permutation(second, total).astype(jnp.int32)
    crowded = jax.random.randint(third, (), 0, OWNERS).astype(jnp.int32)
    places = jnp.arange(total, dtype=jnp.int32)
    scores = jnp.where(places // SLOTS == crowded, places % SLOTS - SLOTS, ranking)
    ordering = jnp.argsort(scores, stable=True)
    table = jnp.full((total,), -1, jnp.int32).at[ordering[:IMPL]].set(chosen)
    return table.reshape(OWNERS, SLOTS)


def set_ends(array, stream_key, least, largest):
    longest = array.shape.index(max(array.shape))
    spots = []
    for shift in (0, 1):
        where = [jax.random.randint(jax.random.fold_in(stream_key, axis), (), 0, length) for axis, length in enumerate(array.shape)]
        where[longest] = (where[longest] + shift) % array.shape[longest]
        spots.append(tuple(where))
    return array.at[spots[0]].set(least).at[spots[1]].set(largest)


def steps_of(rng, shape, pieces, low, largest):
    def one(position, shards_of):
        draws = jax.random.uniform(jax.random.fold_in(jax.random.fold_in(rng, 6), position), (shards_of,), jnp.float32, low / len(pieces), largest / len(pieces))
        return jnp.repeat(jnp.exp(draws), shape[position] // shards_of).reshape((-1,) + (1,) * (len(shape) - position - 1))

    level = one(*pieces[0])
    for cut in pieces[1:]:
        level = level * one(*cut)
    return level


def normal_values(key, dims, deviation, reach, cuts=(), kind=jnp.bfloat16):
    array = jax.random.normal(key, dims, jnp.float32) * deviation
    if len(cuts) > 0:
        array = steps_of(key, dims, cuts, -0.22, 0.18) * array
    return jnp.clip(array, min=-reach, max=reach).astype(kind)


def setup_inputs(seed: int = 0, part: int = 0) -> dict:
    arg_keys = jax.random.split(jax.random.key(seed), 10)
    part_keys = jax.random.split(jax.random.fold_in(arg_keys[9], part), 10)
    return {
        "state": normal_values(part_keys[0], (NLAT, NLON, K), 1.0, 6.0, ((0, 16),), jnp.float32),
        "east_wind": normal_values(part_keys[1], (NLAT, NLON, K), 1.0, 6.0, ((0, 16),), jnp.float32),
        "north_wind": normal_values(part_keys[2], (NLAT, NLON, K), 1.0, 6.0, ((0, 16),), jnp.float32),
        "coef": jnp.clip(jax.random.uniform(part_keys[3], (NLAT, NLON), jnp.float32, 0.5, 2.0), 0.5, 2.0),
        "project": normal_values(arg_keys[4], (K, K), K ** -0.5, 0.5, (), jnp.float32),
        "restore": normal_values(arg_keys[5], (K, K), K ** -0.5, 0.5, (), jnp.float32),
        "stiffness": jnp.clip(jnp.exp(jax.random.uniform(arg_keys[6], (K,), jnp.float32, math.log(4.0), math.log(1000.0))), 4.0, 1000.0),
        "sweeps": set_ends(jax.random.randint(arg_keys[7], (K,), 2, 9), jax.random.fold_in(arg_keys[7], 1), 2, 8).astype(jnp.int32),
        "mode_slots": draw_mode_slots(jax.random.fold_in(jax.random.fold_in(arg_keys[9], part), 71), part),
    }


time_step = 0.2
diffusion = 0.05
coef_top = 2.0
sweep_limit = 8
highest = lax.Precision.HIGHEST


def tendency(state, padded, east_wind, north_wind):
    northern = padded[2:]
    southern = padded[:-2]
    eastern = jnp.roll(state, -1, 1)
    western = jnp.roll(state, 1, 1)
    advect = east_wind * (eastern - western) * 0.5 + north_wind * (northern - southern) * 0.5
    spread = eastern + western + northern + southern - 4.0 * state
    return state - time_step * advect + time_step * diffusion * spread


def helmholtz(field, coef, weight_slot):
    padded = jnp.pad(field, ((0, 0), (1, 1), (0, 0)))
    northern = padded[:, 2:, :]
    southern = padded[:, :-2, :]
    eastern = jnp.roll(field, -1, 2)
    western = jnp.roll(field, 1, 2)
    corners = jnp.roll(northern, -1, 2) + jnp.roll(northern, 1, 2) + jnp.roll(southern, -1, 2) + jnp.roll(southern, 1, 2)
    laplace = (4.0 * (northern + southern + eastern + western) + corners - 20.0 * field) / 6.0
    return field - weight_slot * coef * laplace


def chebyshev(source, coef, weights, counts, length):
    upper = 1.0 + weights * (coef_top * 16.0 / 3.0)
    centre = ((upper + 1.0) * 0.5)[:, None, None]
    radius = ((upper - 1.0) * 0.5)[:, None, None]
    ratio = centre / radius
    weight_slot = weights[:, None, None]

    def sweep(index, carry):
        iterate, residual, direction, factor = carry
        image = helmholtz(direction, coef, weight_slot)
        next_factor = 1.0 / (2.0 * ratio - factor)
        new_iterate = iterate + direction
        new_residual = residual - image
        new_direction = next_factor * factor * direction + (2.0 * next_factor / radius) * new_residual
        active = (index < counts)[:, None, None]
        return (jnp.where(active, new_iterate, iterate), jnp.where(active, new_residual, residual),
                jnp.where(active, new_direction, direction), jnp.where(active, next_factor, factor))

    start = (jnp.zeros_like(source), source, source / centre, 1.0 / ratio)
    return lax.fori_loop(0, length, sweep, start)[0]


def reference(state, east_wind, north_wind, coef, project, restore, stiffness, sweeps, mode_slots):
    padded = jnp.pad(state, ((1, 1), (0, 0), (0, 0)))
    forcing = tendency(state, padded, east_wind, north_wind)
    rows, lons, levels = forcing.shape
    modes = jnp.dot(forcing.reshape(-1, levels), project, precision=highest, preferred_element_type=jnp.float32)
    fields = jnp.transpose(modes.reshape(rows, lons, levels), (2, 0, 1))
    listed_ids = mode_slots.reshape(-1)
    mode_range = jnp.arange(levels, dtype=jnp.int32)
    listed = jnp.any(listed_ids[:, None] == mode_range[None, :], axis=0)
    counts = jnp.where(listed, sweeps, 0)
    solved = chebyshev(fields, coef, stiffness, counts, sweep_limit)
    final = jnp.where(listed[:, None, None], solved, fields)
    columns = jnp.transpose(final, (1, 2, 0)).reshape(-1, levels)
    result = jnp.dot(columns, restore, precision=highest, preferred_element_type=jnp.float32)
    return result.reshape(rows, lons, levels)
```

```python
import functools

import jax
import jax.numpy as jnp
from jax import lax
from jax.experimental import pallas as pl
from jax.experimental.pallas import tpu as pltpu
from jax.sharding import PartitionSpec as P

time_step = 0.2
diffusion = 0.05
coef_top = 2.0
sweep_limit = 8
highest = lax.Precision.HIGHEST
MESH = pl.DeviceIdType.MESH
f32 = jnp.float32
bf16 = jnp.bfloat16

REACH = sweep_limit - 1
WINDOW = 2 * REACH + 2
OFFSETS = (1, -1, 2, -2, 3, -3, 4, -4)
VMEM_LIMIT = 48 * 1024 * 1024

NN = (((1,), (0,)), ((), ()))
NT = (((1,), (1,)), ((), ()))
TN = (((0,), (0,)), ((), ()))


def split(x):
    high = x.astype(bf16)
    return high, (x - high.astype(f32)).astype(bf16)


def dot3(a, b, dims):
    (ah, al), (bh, bl) = a, b
    product = functools.partial(lax.dot_general, dimension_numbers=dims, preferred_element_type=f32)
    return product(ah, bh) + (product(ah, bl) + product(al, bh))


def kernel(devices, full, tail, state, east_wind, north_wind, coef, project, restore, stiffness, sweeps,
           mode_slots, out, sv, ev, nv, cv, pv, rv, stv, swv, msv, south, north, own, window, dir_a,
           dir_b, weight, gain, fh, fl, load_sem, halo_send, halo_recv, mode_send, mode_recv):
    me = lax.axis_index("lat")
    rows, lons, levels = state.shape
    nlat = coef.shape[0]
    half = lons // 2
    ranks = 8 * (full + tail)
    core = lax.rem(me, 2)
    chip, chips = me // 2, devices // 2

    loads = [
        pltpu.make_async_copy(source, target, load_sem.at[i])
        for i, (source, target) in enumerate((
            (state, sv), (east_wind, ev), (north_wind, nv), (project, pv), (restore, rv),
            (mode_slots, msv), (stiffness, stv), (sweeps, swv), (coef, cv)))
    ]
    for load in loads:
        load.start()

    barrier = pltpu.get_barrier_semaphore()
    for offset in OFFSETS:
        @pl.when((me + offset >= 0) & (me + offset < devices))
        def _(offset=offset):
            pl.semaphore_signal(barrier, inc=1, device_id={"lat": me + offset}, device_id_type=MESH)
    pl.semaphore_wait(barrier, jnp.minimum(me, 4) + jnp.minimum(devices - 1 - me, 4))

    def halo(way):
        return pltpu.make_async_remote_copy(
            src_ref=state.at[1 - way], dst_ref=(south, north)[way],
            send_sem=halo_send.at[way], recv_sem=halo_recv.at[way],
            device_id={"lat": me + 1 - 2 * way}, device_id_type=MESH)

    has_north = me < devices - 1
    has_south = me > 0

    @pl.when(has_north)
    def _():
        halo(0).start()

    @pl.when(has_south)
    def _():
        halo(1).start()

    @pl.when(jnp.logical_not(has_south))
    def _():
        south[...] = jnp.zeros_like(south)

    @pl.when(jnp.logical_not(has_north))
    def _():
        north[...] = jnp.zeros_like(north)

    for w in range(WINDOW):
        at = 2 * me - REACH + w

        @pl.when((at < 0) | (at >= nlat))
        def _(w=w):
            window[w] = jnp.zeros(window.shape[1:], f32)

    for load in loads[:3]:
        load.wait()
    for row in range(rows):
        here, other = sv[row], sv[1 - row]
        east = pltpu.roll(here, lons - 1, 0)
        west = pltpu.roll(here, 1, 0)
        wind = nv[row] * (0.5 * time_step)
        sign = 1.0 if row == 0 else -1.0
        ev[row] = (here - (0.5 * time_step) * ev[row] * (east - west) - sign * wind * other
                   + (time_step * diffusion) * (east + west + other - 4.0 * here))
        nv[row] = sign * wind + time_step * diffusion

    for load in loads[3:]:
        load.wait()
    number = lax.broadcasted_iota(jnp.int32, (levels, mode_slots.shape[1]), 0)
    hit = jnp.zeros(number.shape, f32)
    for slot in range(mode_slots.shape[0]):
        hit = jnp.maximum(hit, jnp.where(msv[slot:slot + 1, :] == number, 1.0, 0.0))
    hit = jnp.max(hit, axis=1, keepdims=True)
    listed = jnp.transpose(jnp.broadcast_to(hit, (levels, levels)))[0:1]
    before = lax.broadcasted_iota(jnp.int32, (levels, levels), 0) < lax.broadcasted_iota(
        jnp.int32, (levels, levels), 1)
    rank = lax.dot_general(
        jnp.broadcast_to(listed, (8, levels)).astype(bf16), jnp.where(before, 1.0, 0.0).astype(bf16),
        NN, preferred_element_type=f32)[0:1]
    place = lax.broadcasted_iota(jnp.int32, (ranks, levels), 0)
    place = jnp.where(place < 8 * full + 4, place, place - 4 * tail)
    chosen = jnp.where(rank == place.astype(f32), 1.0, 0.0) * listed
    used = jnp.sum(chosen, axis=1, keepdims=True)
    weights = jnp.sum(chosen * stv[...], axis=1, keepdims=True) + (1.0 - used)
    counts = jnp.sum(chosen * swv[...].astype(f32), axis=1, keepdims=True)
    project_sel = split(lax.dot_general(chosen, pv[...], NT, precision=highest, preferred_element_type=f32))
    restore_sel = split(lax.dot_general(chosen, rv[...], NN, precision=highest, preferred_element_type=f32))
    both = split(lax.dot_general(pv[...], rv[...], NN, precision=highest, preferred_element_type=f32))

    upper = 1.0 + weights * (coef_top * 16.0 / 3.0)
    centre = (upper + 1.0) * 0.5
    radius = (upper - 1.0) * 0.5
    ratio = centre / radius
    factor = 1.0 / ratio
    wide = (ranks, 128)
    gain[2 * REACH] = jnp.broadcast_to(1.0 / centre, wide)
    for k in range(REACH):
        next_factor = 1.0 / (2.0 * ratio - factor)
        gain[2 * k] = jnp.broadcast_to(next_factor * factor, wide)
        gain[2 * k + 1] = jnp.broadcast_to(2.0 * next_factor / radius, wide)
        factor = next_factor
    gain[2 * REACH + 1] = jnp.broadcast_to(counts, wide)
    sixth = weights / 6.0

    upper_half = lax.broadcasted_iota(jnp.int32, (8, half), 0) < 4
    groups = [(slice(8 * g, 8 * g + 8), slice(g * lons, (g + 1) * lons), False) for g in range(full)]
    if tail:
        groups.append((slice(8 * full, 8 * full + 8), slice(full * lons, full * lons + half), True))

    for w in range(1, WINDOW - 1):
        at = 2 * me - REACH + w
        inside = jnp.where((at >= 0) & (at < nlat), 1.0, 0.0)
        line = cv[pl.ds(jnp.clip(at, 0, nlat - 1), 1), :] * inside
        for part, lanes, is_tail in groups:
            if is_tail:
                weight[w - 1, :, lanes] = sixth[part] * jnp.where(upper_half, line[:, :half], line[:, half:])
            else:
                weight[w - 1, :, lanes] = sixth[part] * line

    def copy(index, source, first, count, target_row, target):
        return pltpu.make_async_remote_copy(
            src_ref=source.at[pl.ds(first, count)], dst_ref=window.at[pl.ds(target_row, count)],
            send_sem=mode_send.at[index], recv_sem=mode_recv.at[index],
            device_id={"lat": target}, device_id_type=MESH)

    sibling = me + 1 - 2 * core
    low1, low2, high1, high2 = chip >= 1, chip >= 2, chip + 1 < chips, chip + 2 < chips
    near = ((core == 0) & low2) | ((core == 1) & high2)
    far = ((core == 1) & low2) | ((core == 0) & high2)
    always = me >= 0
    sends = (
        (lambda: copy(3, own, 1, 1, 0, me + 4), high2, low2),
        (lambda: copy(4, own, 0, 1, WINDOW - 1, me - 4), low2, high2),
        (lambda: copy(5, own, 1 - core, 1, 14 - 13 * core, me - 3 + 6 * core), near, near),
        (lambda: copy(1, own, 0, 2, 3, me + 2), high1, low1),
        (lambda: copy(2, own, 0, 2, 11, me - 2), low1, high1),
        (lambda: copy(0, own, 0, 2, 5 + 4 * core, sibling), always, always),
    )
    relays = (
        (lambda: copy(6, window, 3, 2, 1 + 4 * core, sibling), low1, low1, (3,)),
        (lambda: copy(7, window, 11, 2, 9 + 4 * core, sibling), high1, high1, (4,)),
        (lambda: copy(8, window, 15 - 15 * core, 1, 13 - 11 * core, sibling), far, near, (0, 1)),
    )

    for row in range(rows):
        @pl.when((has_south, has_north)[row])
        def _(row=row):
            halo(row).wait_recv()
        forcing = ev[row] + nv[row] * (south, north)[row][...]
        pieces = split(forcing)
        fh[row], fl[row] = pieces
        modes = dot3(project_sel, pieces, NT)
        for part, lanes, is_tail in groups:
            field = modes[part]
            if is_tail:
                field = jnp.where(upper_half, field[:, :half], field[:, half:])
            own[row, :, lanes] = field
            window[REACH + row, :, lanes] = field

    for start, sent, _ in sends[3:5] + sends[:3] + sends[5:]:
        @pl.when(sent)
        def _(start=start):
            start().start()

    out[0] = dot3((fh[0], fl[0]), both, NN)
    for start, sent, _, needs in relays:
        for need in needs:
            @pl.when(sends[need][2])
            def _(need=need):
                sends[need][0]().wait_recv()

        @pl.when(sent)
        def _(start=start):
            start().start()
    out[1] = dot3((fh[1], fl[1]), both, NN)
    for start, _, received in (sends[2], sends[5]) + tuple(relay[:3] for relay in relays):
        @pl.when(received)
        def _(start=start):
            start().wait_recv()

    for start, sent in [entry[:2] for entry in relays]:
        @pl.when(sent)
        def _(start=start):
            start().wait_send()

    for part, lanes, is_tail in groups:
        lon = half if is_tail else lons

        def spread(value):
            return jnp.concatenate([value] * (lon // 128), axis=1)

        def shifted(value, by):
            moved = pltpu.roll(value, by % lon, 1)
            if not is_tail:
                return moved
            edge = lax.broadcasted_iota(jnp.int32, (8, lon), 1) == (0 if by == 1 else lon - 1)
            return jnp.where(edge, pltpu.roll(moved, 4, 0), moved)

        inverse = spread(gain[2 * REACH, part])
        limit = spread(gain[2 * REACH + 1, part])
        for w in range(WINDOW):
            dir_a[w, :, :lon] = window[w, :, lanes] * inverse
        totals = [dir_a[REACH, :, :lon], dir_a[REACH + 1, :, :lon]]
        now, later = dir_a, dir_b
        for k in range(REACH):
            keep, push = spread(gain[2 * k, part]), spread(gain[2 * k + 1, part])
            for w in range(k + 1, WINDOW - 1 - k):
                here = now[w, :, :lon]
                sides = now[w - 1, :, :lon] + now[w + 1, :, :lon]
                mixed = 4.0 * here + sides
                laplace = shifted(mixed, 1) + shifted(mixed, -1) + (4.0 * sides - 20.0 * here)
                residual = window[w, :, lanes] - (here - weight[w - 1, :, lanes] * laplace)
                if k < REACH - 1:
                    window[w, :, lanes] = residual
                fresh = keep * here + push * residual
                later[w, :, :lon] = fresh
                if REACH <= w < REACH + 2:
                    totals[w - REACH] += jnp.where(k + 1 < limit, fresh, 0.0)
            now, later = later, now
        few = tuple(piece[part] for piece in restore_sel)
        for row in range(rows):
            change = totals[row] - own[row, :, lanes]
            if is_tail:
                change = jnp.concatenate(
                    [jnp.where(upper_half, change, 0.0), jnp.where(upper_half, 0.0, change)], axis=1)
            out[row] += dot3(split(change), few, TN)

    @pl.when(has_north)
    def _():
        halo(0).wait_send()

    @pl.when(has_south)
    def _():
        halo(1).wait_send()
    for start, sent in [entry[:2] for entry in sends]:
        @pl.when(sent)
        def _(start=start):
            start().wait_send()


def solution(mesh):
    devices = mesh.shape["lat"]

    def local(state, east_wind, north_wind, coef, project, restore, stiffness, sweeps, mode_slots):
        rows, lons, levels = state.shape
        nlat = coef.shape[0]
        listed = mode_slots.shape[0] * mode_slots.shape[1] * 3 // 8
        full, rest = listed // 8, listed % 8
        tail = 1 if rest == 4 else 0
        full += 1 if rest and not tail else 0
        ranks = 8 * (full + tail)
        packed = full * lons + tail * lons // 2
        anywhere = pl.BlockSpec(memory_space=pl.ANY)
        vmem = pltpu.VMEM
        block = vmem((rows, lons, levels), f32)
        return pl.pallas_call(
            functools.partial(kernel, devices, full, tail),
            out_shape=pltpu.VMEM(state.shape, f32),
            in_specs=[anywhere] * 9,
            out_specs=pl.BlockSpec(memory_space=pltpu.VMEM),
            scratch_shapes=[
                block, block, block,
                vmem(coef.shape, f32), vmem(project.shape, f32), vmem(restore.shape, f32),
                vmem((1, levels), f32), vmem((1, levels), jnp.int32),
                vmem(mode_slots.shape[::-1], jnp.int32),
                vmem((lons, levels), f32), vmem((lons, levels), f32),
                vmem((rows, 8, packed), f32), vmem((WINDOW, 8, packed), f32),
                vmem((WINDOW, 8, lons), f32), vmem((WINDOW, 8, lons), f32),
                vmem((WINDOW - 2, 8, packed), f32), vmem((2 * REACH + 2, ranks, 128), f32),
                vmem((rows, lons, levels), bf16), vmem((rows, lons, levels), bf16),
                pltpu.SemaphoreType.DMA((9,)),
                pltpu.SemaphoreType.DMA((2,)), pltpu.SemaphoreType.DMA((2,)),
                pltpu.SemaphoreType.DMA((9,)), pltpu.SemaphoreType.DMA((9,)),
            ],
            compiler_params=pltpu.CompilerParams(
                collective_id=0, has_side_effects=True, vmem_limit_bytes=VMEM_LIMIT),
        )(state, east_wind, north_wind, coef, project, restore, stiffness.reshape(1, levels),
          sweeps.reshape(1, levels), mode_slots.T)

    placed = (
        P(("parts", "lat"), None, None),
        P(("parts", "lat"), None, None),
        P(("parts", "lat"), None, None),
        P("parts", None),
        P(),
        P(),
        P(),
        P(),
        P("parts", None),
    )
    return jax.shard_map(
        local,
        mesh=mesh,
        in_specs=placed,
        out_specs=P(("parts", "lat"), None, None),
        check_vma=False,
    )
```

```python
import functools

import jax
import jax.numpy as jnp
from jax import lax
from jax.experimental import pallas as pl
from jax.experimental.pallas import tpu as pltpu
from jax.sharding import PartitionSpec as P

time_step = 0.2
diffusion = 0.05
coef_top = 2.0
sweep_limit = 8
highest = lax.Precision.HIGHEST
MESH = pl.DeviceIdType.MESH
f32 = jnp.float32
bf16 = jnp.bfloat16

REACH = sweep_limit - 1
WINDOW = 2 * REACH + 2
OFFSETS = (1, -1, 2, -2, 3, -3, 4, -4)
VMEM_LIMIT = 60 * 1024 * 1024

NN = (((1,), (0,)), ((), ()))
NT = (((1,), (1,)), ((), ()))
TN = (((0,), (0,)), ((), ()))


def split(x):
    high = x.astype(bf16)
    return high, (x - high.astype(f32)).astype(bf16)


def dot3(a, b, dims):
    (ah, al), (bh, bl) = a, b
    product = functools.partial(lax.dot_general, dimension_numbers=dims, preferred_element_type=f32)
    return product(ah, bh) + (product(ah, bl) + product(al, bh))


def kernel(devices, full, tail, state, east_wind, north_wind, coef, project, restore, stiffness, sweeps,
           mode_slots, out, sv, ev, nv, cv, pv, rv, stv, swv, msv, south, north, own, window, dir_a,
           dir_b, weight, gain, fh, fl, load_sem, halo_send, halo_recv, mode_send, mode_recv):
    me = lax.axis_index("lat")
    rows, lons, levels = state.shape
    nlat = coef.shape[0]
    half = lons // 2
    ranks = 8 * (full + tail)
    core = lax.rem(me, 2)
    chip, chips = me // 2, devices // 2

    loads = [
        pltpu.make_async_copy(source, target, load_sem.at[i])
        for i, (source, target) in enumerate((
            (state, sv), (east_wind, ev), (north_wind, nv), (project, pv), (restore, rv),
            (mode_slots, msv), (stiffness, stv), (sweeps, swv), (coef, cv)))
    ]
    for load in loads:
        load.start()

    barrier = pltpu.get_barrier_semaphore()
    for offset in OFFSETS:
        @pl.when((me + offset >= 0) & (me + offset < devices))
        def _(offset=offset):
            pl.semaphore_signal(barrier, inc=1, device_id={"lat": me + offset}, device_id_type=MESH)
    pl.semaphore_wait(barrier, jnp.minimum(me, 4) + jnp.minimum(devices - 1 - me, 4))

    def halo(way):
        return pltpu.make_async_remote_copy(
            src_ref=state.at[1 - way], dst_ref=(south, north)[way],
            send_sem=halo_send.at[way], recv_sem=halo_recv.at[way],
            device_id={"lat": me + 1 - 2 * way}, device_id_type=MESH)

    has_north = me < devices - 1
    has_south = me > 0

    @pl.when(has_north)
    def _():
        halo(0).start()

    @pl.when(has_south)
    def _():
        halo(1).start()

    @pl.when(jnp.logical_not(has_south))
    def _():
        south[...] = jnp.zeros_like(south)

    @pl.when(jnp.logical_not(has_north))
    def _():
        north[...] = jnp.zeros_like(north)

    for w in range(WINDOW):
        at = 2 * me - REACH + w

        @pl.when((at < 0) | (at >= nlat))
        def _(w=w):
            window[w] = jnp.zeros(window.shape[1:], f32)

    for load in loads[:3]:
        load.wait()
    for row in range(rows):
        here, other = sv[row], sv[1 - row]
        east = pltpu.roll(here, lons - 1, 0)
        west = pltpu.roll(here, 1, 0)
        wind = nv[row] * (0.5 * time_step)
        sign = 1.0 if row == 0 else -1.0
        ev[row] = (here - (0.5 * time_step) * ev[row] * (east - west) - sign * wind * other
                   + (time_step * diffusion) * (east + west + other - 4.0 * here))
        nv[row] = sign * wind + time_step * diffusion

    for load in loads[3:]:
        load.wait()
    number = lax.broadcasted_iota(jnp.int32, (levels, mode_slots.shape[1]), 0)
    hit = jnp.zeros(number.shape, f32)
    for slot in range(mode_slots.shape[0]):
        hit = jnp.maximum(hit, jnp.where(msv[slot:slot + 1, :] == number, 1.0, 0.0))
    hit = jnp.max(hit, axis=1, keepdims=True)
    listed = jnp.transpose(jnp.broadcast_to(hit, (levels, levels)))[0:1]
    before = lax.broadcasted_iota(jnp.int32, (levels, levels), 0) < lax.broadcasted_iota(
        jnp.int32, (levels, levels), 1)
    rank = lax.dot_general(
        jnp.broadcast_to(listed, (8, levels)).astype(bf16), jnp.where(before, 1.0, 0.0).astype(bf16),
        NN, preferred_element_type=f32)[0:1]
    place = lax.broadcasted_iota(jnp.int32, (ranks, levels), 0)
    place = jnp.where(place < 8 * full + 4, place, place - 4 * tail)
    chosen = jnp.where(rank == place.astype(f32), 1.0, 0.0) * listed
    used = jnp.sum(chosen, axis=1, keepdims=True)
    weights = jnp.sum(chosen * stv[...], axis=1, keepdims=True) + (1.0 - used)
    counts = jnp.sum(chosen * swv[...].astype(f32), axis=1, keepdims=True)
    project_sel = split(lax.dot_general(chosen, pv[...], NT, precision=highest, preferred_element_type=f32))
    restore_sel = split(lax.dot_general(chosen, rv[...], NN, precision=highest, preferred_element_type=f32))
    both = split(lax.dot_general(pv[...], rv[...], NN, precision=highest, preferred_element_type=f32))

    upper = 1.0 + weights * (coef_top * 16.0 / 3.0)
    centre = (upper + 1.0) * 0.5
    radius = (upper - 1.0) * 0.5
    ratio = centre / radius
    factor = 1.0 / ratio
    wide = (ranks, 128)
    gain[2 * REACH] = jnp.broadcast_to(1.0 / centre, wide)
    for k in range(REACH):
        next_factor = 1.0 / (2.0 * ratio - factor)
        gain[2 * k] = jnp.broadcast_to(next_factor * factor, wide)
        gain[2 * k + 1] = jnp.broadcast_to(2.0 * next_factor / radius, wide)
        factor = next_factor
    gain[2 * REACH + 1] = jnp.broadcast_to(counts, wide)
    sixth = weights / 6.0

    upper_half = lax.broadcasted_iota(jnp.int32, (8, half), 0) < 4
    groups = [(slice(8 * g, 8 * g + 8), slice(g * lons, (g + 1) * lons), False) for g in range(full)]
    if tail:
        groups.append((slice(8 * full, 8 * full + 8), slice(full * lons, full * lons + half), True))

    for w in range(1, WINDOW - 1):
        at = 2 * me - REACH + w
        inside = jnp.where((at >= 0) & (at < nlat), 1.0, 0.0)
        line = cv[pl.ds(jnp.clip(at, 0, nlat - 1), 1), :] * inside
        for part, lanes, is_tail in groups:
            if is_tail:
                weight[w - 1, :, lanes] = sixth[part] * jnp.where(upper_half, line[:, :half], line[:, half:])
            else:
                weight[w - 1, :, lanes] = sixth[part] * line

    def copy(index, source, first, count, target_row, target):
        return pltpu.make_async_remote_copy(
            src_ref=source.at[pl.ds(first, count)], dst_ref=window.at[pl.ds(target_row, count)],
            send_sem=mode_send.at[index], recv_sem=mode_recv.at[index],
            device_id={"lat": target}, device_id_type=MESH)

    sibling = me + 1 - 2 * core
    low1, low2, high1, high2 = chip >= 1, chip >= 2, chip + 1 < chips, chip + 2 < chips
    near = ((core == 0) & low2) | ((core == 1) & high2)
    far = ((core == 1) & low2) | ((core == 0) & high2)
    always = me >= 0
    sends = (
        (lambda: copy(3, own, 1, 1, 0, me + 4), high2, low2),
        (lambda: copy(4, own, 0, 1, WINDOW - 1, me - 4), low2, high2),
        (lambda: copy(5, own, 1 - core, 1, 14 - 13 * core, me - 3 + 6 * core), near, near),
        (lambda: copy(1, own, 0, 2, 3, me + 2), high1, low1),
        (lambda: copy(2, own, 0, 2, 11, me - 2), low1, high1),
        (lambda: copy(0, own, 0, 2, 5 + 4 * core, sibling), always, always),
    )
    relays = (
        (lambda: copy(6, window, 3, 2, 1 + 4 * core, sibling), low1, low1, (3,)),
        (lambda: copy(7, window, 11, 2, 9 + 4 * core, sibling), high1, high1, (4,)),
        (lambda: copy(8, window, 15 - 15 * core, 1, 13 - 11 * core, sibling), far, near, (0, 1)),
    )

    for row in range(rows):
        @pl.when((has_south, has_north)[row])
        def _(row=row):
            halo(row).wait_recv()
        forcing = ev[row] + nv[row] * (south, north)[row][...]
        pieces = split(forcing)
        fh[row], fl[row] = pieces
        modes = dot3(project_sel, pieces, NT)
        for part, lanes, is_tail in groups:
            field = modes[part]
            if is_tail:
                field = jnp.where(upper_half, field[:, :half], field[:, half:])
            own[row, :, lanes] = field
            window[REACH + row, :, lanes] = field

    for start, sent, _ in sends[3:5] + sends[:3] + sends[5:]:
        @pl.when(sent)
        def _(start=start):
            start().start()

    out[0] = dot3((fh[0], fl[0]), both, NN)
    for start, sent, _, needs in relays:
        for need in needs:
            @pl.when(sends[need][2])
            def _(need=need):
                sends[need][0]().wait_recv()

        @pl.when(sent)
        def _(start=start):
            start().start()
    out[1] = dot3((fh[1], fl[1]), both, NN)
    for start, _, received in (sends[2], sends[5]) + tuple(relay[:3] for relay in relays):
        @pl.when(received)
        def _(start=start):
            start().wait_recv()

    for start, sent in [entry[:2] for entry in relays]:
        @pl.when(sent)
        def _(start=start):
            start().wait_send()

    for part, lanes, is_tail in groups:
        lon = half if is_tail else lons

        def spread(value):
            return jnp.concatenate([value] * (lon // 128), axis=1)

        def shifted(value, by):
            moved = pltpu.roll(value, by % lon, 1)
            if not is_tail:
                return moved
            edge = lax.broadcasted_iota(jnp.int32, (8, lon), 1) == (0 if by == 1 else lon - 1)
            return jnp.where(edge, pltpu.roll(moved, 4, 0), moved)

        inverse = spread(gain[2 * REACH, part])
        limit = spread(gain[2 * REACH + 1, part])
        for w in range(WINDOW):
            dir_a[w, :, :lon] = window[w, :, lanes] * inverse
        totals = [dir_a[REACH, :, :lon], dir_a[REACH + 1, :, :lon]]
        now, later = dir_a, dir_b
        for k in range(REACH):
            keep, push = spread(gain[2 * k, part]), spread(gain[2 * k + 1, part])
            for w in range(k + 1, WINDOW - 1 - k):
                here = now[w, :, :lon]
                sides = now[w - 1, :, :lon] + now[w + 1, :, :lon]
                mixed = 4.0 * here + sides
                laplace = shifted(mixed, 1) + shifted(mixed, -1) + (4.0 * sides - 20.0 * here)
                residual = window[w, :, lanes] - (here - weight[w - 1, :, lanes] * laplace)
                if k < REACH - 1:
                    window[w, :, lanes] = residual
                fresh = keep * here + push * residual
                later[w, :, :lon] = fresh
                if REACH <= w < REACH + 2:
                    totals[w - REACH] += jnp.where(k + 1 < limit, fresh, 0.0)
            now, later = later, now
        few = tuple(piece[part] for piece in restore_sel)
        for row in range(rows):
            change = totals[row] - own[row, :, lanes]
            if is_tail:
                change = jnp.concatenate(
                    [jnp.where(upper_half, change, 0.0), jnp.where(upper_half, 0.0, change)], axis=1)
            out[row] += dot3(split(change), few, TN)

    @pl.when(has_north)
    def _():
        halo(0).wait_send()

    @pl.when(has_south)
    def _():
        halo(1).wait_send()
    for start, sent in [entry[:2] for entry in sends]:
        @pl.when(sent)
        def _(start=start):
            start().wait_send()


def solution(mesh):
    devices = mesh.shape["lat"]

    def local(state, east_wind, north_wind, coef, project, restore, stiffness, sweeps, mode_slots):
        rows, lons, levels = state.shape
        nlat = coef.shape[0]
        listed = mode_slots.shape[0] * mode_slots.shape[1] * 3 // 8
        full, rest = listed // 8, listed % 8
        tail = 1 if rest == 4 else 0
        full += 1 if rest and not tail else 0
        ranks = 8 * (full + tail)
        packed = full * lons + tail * lons // 2
        anywhere = pl.BlockSpec(memory_space=pl.ANY)
        vmem = pltpu.VMEM
        block = vmem((rows, lons, levels), f32)
        return pl.pallas_call(
            functools.partial(kernel, devices, full, tail),
            out_shape=pltpu.VMEM(state.shape, f32),
            in_specs=[anywhere] * 9,
            out_specs=pl.BlockSpec(memory_space=pltpu.VMEM),
            scratch_shapes=[
                block, block, block,
                vmem(coef.shape, f32), vmem(project.shape, f32), vmem(restore.shape, f32),
                vmem((1, levels), f32), vmem((1, levels), jnp.int32),
                vmem(mode_slots.shape[::-1], jnp.int32),
                vmem((lons, levels), f32), vmem((lons, levels), f32),
                vmem((rows, 8, packed), f32), vmem((WINDOW, 8, packed), f32),
                vmem((WINDOW, 8, lons), f32), vmem((WINDOW, 8, lons), f32),
                vmem((WINDOW - 2, 8, packed), f32), vmem((2 * REACH + 2, ranks, 128), f32),
                vmem((rows, lons, levels), bf16), vmem((rows, lons, levels), bf16),
                pltpu.SemaphoreType.DMA((9,)),
                pltpu.SemaphoreType.DMA((2,)), pltpu.SemaphoreType.DMA((2,)),
                pltpu.SemaphoreType.DMA((9,)), pltpu.SemaphoreType.DMA((9,)),
            ],
            compiler_params=pltpu.CompilerParams(
                collective_id=0, has_side_effects=True, vmem_limit_bytes=VMEM_LIMIT),
        )(state, east_wind, north_wind, coef, project, restore, stiffness.reshape(1, levels),
          sweeps.reshape(1, levels), mode_slots.T)

    placed = (
        P(("parts", "lat"), None, None),
        P(("parts", "lat"), None, None),
        P(("parts", "lat"), None, None),
        P("parts", None),
        P(),
        P(),
        P(),
        P(),
        P("parts", None),
    )
    return jax.shard_map(
        local,
        mesh=mesh,
        in_specs=placed,
        out_specs=P(("parts", "lat"), None, None),
        check_vma=False,
    )
```

```python
import functools

import jax
import jax.numpy as jnp
from jax import lax
from jax.experimental import pallas as pl
from jax.experimental.pallas import tpu as pltpu
from jax.sharding import PartitionSpec as P

time_step = 0.2
diffusion = 0.05
coef_top = 2.0
sweep_limit = 8
highest = lax.Precision.HIGHEST
MESH = pl.DeviceIdType.MESH
f32 = jnp.float32
bf16 = jnp.bfloat16

REACH = sweep_limit - 1
WINDOW = 2 * REACH + 2
OFFSETS = (1, -1, 2, -2, 3, -3, 4, -4)
VMEM_LIMIT = 60 * 1024 * 1024

NN = (((1,), (0,)), ((), ()))
NT = (((1,), (1,)), ((), ()))
TN = (((0,), (0,)), ((), ()))


def split(x):
    high = x.astype(bf16)
    return high, (x - high.astype(f32)).astype(bf16)


def dot3(a, b, dims):
    (ah, al), (bh, bl) = a, b
    product = functools.partial(lax.dot_general, dimension_numbers=dims, preferred_element_type=f32)
    return product(ah, bh) + (product(ah, bl) + product(al, bh))


def kernel(devices, full, tail, state, east_wind, north_wind, coef, project, restore, stiffness, sweeps,
           mode_slots, out, sv, ev, nv, cv, pv, rv, stv, swv, msv, outer_halo, inner_halo, own, window, dir_a,
           dir_b, left, weight, gain, fh, fl, load_sem, halo_send, halo_recv, mode_send, mode_recv):
    me = lax.axis_index("lat")
    rows, lons, levels = state.shape
    nlat = coef.shape[0]
    half = lons // 2
    ranks = 8 * (full + tail)
    core = lax.rem(me, 2)
    chip, chips = me // 2, devices // 2
    tiles = lons // 128
    chunks = tiles // 2
    width = (2 * full + tail) * 128
    packed = chunks * width
    inner, outer = 1 - core, core

    loads = [
        pltpu.make_async_copy(source, target, load_sem.at[i])
        for i, (source, target) in enumerate((
            (state, sv), (east_wind, ev), (north_wind, nv), (project, pv), (restore, rv),
            (mode_slots, msv), (stiffness, stv), (sweeps, swv), (coef, cv)))
    ]
    for load in loads:
        load.start()

    barrier = pltpu.get_barrier_semaphore()
    for offset in OFFSETS:
        @pl.when((me + offset >= 0) & (me + offset < devices))
        def _(offset=offset):
            pl.semaphore_signal(barrier, inc=1, device_id={"lat": me + offset}, device_id_type=MESH)
    pl.semaphore_wait(barrier, jnp.minimum(me, 4) + jnp.minimum(devices - 1 - me, 4))

    low1, low2, high1, high2 = chip >= 1, chip >= 2, chip + 1 < chips, chip + 2 < chips
    is0, is1 = core == 0, core == 1
    always = me >= 0
    sibling = me + 1 - 2 * core
    beyond = me - 1 + 2 * core
    has_beyond = (is0 & low1) | (is1 & high1)

    def halo(tile):
        span = pl.ds(tile * 128, 128)
        return pltpu.make_async_remote_copy(
            src_ref=state.at[outer, span], dst_ref=outer_halo.at[span],
            send_sem=halo_send.at[tile], recv_sem=halo_recv.at[tile],
            device_id={"lat": beyond}, device_id_type=MESH)

    between = pltpu.make_async_remote_copy(
        src_ref=state.at[inner], dst_ref=inner_halo,
        send_sem=halo_send.at[tiles], recv_sem=halo_recv.at[tiles],
        device_id={"lat": sibling}, device_id_type=MESH)

    @pl.when(has_beyond)
    def _():
        for chunk in range(chunks):
            halo(chunk).start()
            halo(chunk + chunks).start()

    between.start()

    @pl.when(jnp.logical_not(has_beyond))
    def _():
        outer_halo[...] = jnp.zeros_like(outer_halo)

    for w in range(WINDOW):
        at = 2 * me - REACH + w

        @pl.when((at < 0) | (at >= nlat))
        def _(w=w):
            window[w] = jnp.zeros(window.shape[1:], f32)

    for load in loads[:3]:
        load.wait()
    sign0 = (0.5 * time_step) * (2 * core - 1).astype(f32)
    for row, sign in ((inner, sign0), (outer, -sign0)):
        here, other = sv[row], sv[1 - row]
        east = pltpu.roll(here, lons - 1, 0)
        west = pltpu.roll(here, 1, 0)
        wind = nv[row] * sign
        ev[row] = (here - (0.5 * time_step) * ev[row] * (east - west) - wind * other
                   + (time_step * diffusion) * (east + west + other - 4.0 * here))
        nv[row] = wind + time_step * diffusion

    for load in loads[3:]:
        load.wait()
    number = lax.broadcasted_iota(jnp.int32, (levels, mode_slots.shape[1]), 0)
    hit = jnp.zeros(number.shape, f32)
    for slot in range(mode_slots.shape[0]):
        hit = jnp.maximum(hit, jnp.where(msv[slot:slot + 1, :] == number, 1.0, 0.0))
    hit = jnp.max(hit, axis=1, keepdims=True)
    listed = jnp.transpose(jnp.broadcast_to(hit, (levels, levels)))[0:1]
    before = lax.broadcasted_iota(jnp.int32, (levels, levels), 0) < lax.broadcasted_iota(
        jnp.int32, (levels, levels), 1)
    rank = lax.dot_general(
        jnp.broadcast_to(listed, (8, levels)).astype(bf16), jnp.where(before, 1.0, 0.0).astype(bf16),
        NN, preferred_element_type=f32)[0:1]
    place = lax.broadcasted_iota(jnp.int32, (ranks, levels), 0)
    place = jnp.where(place < 8 * full + 4, place, place - 4 * tail)
    chosen = jnp.where(rank == place.astype(f32), 1.0, 0.0) * listed
    used = jnp.sum(chosen, axis=1, keepdims=True)
    weights = jnp.sum(chosen * stv[...], axis=1, keepdims=True) + (1.0 - used)
    counts = jnp.sum(chosen * swv[...].astype(f32), axis=1, keepdims=True)
    project_sel = split(lax.dot_general(chosen, pv[...], NT, precision=highest, preferred_element_type=f32))
    restore_sel = split(lax.dot_general(chosen, rv[...], NN, precision=highest, preferred_element_type=f32))
    both = split(lax.dot_general(pv[...], rv[...], NN, precision=highest, preferred_element_type=f32))

    upper = 1.0 + weights * (coef_top * 16.0 / 3.0)
    centre = (upper + 1.0) * 0.5
    radius = (upper - 1.0) * 0.5
    ratio = centre / radius
    factor = 1.0 / ratio
    wide = (ranks, 128)
    gain[2 * REACH] = jnp.broadcast_to(1.0 / centre, wide)
    for k in range(REACH):
        next_factor = 1.0 / (2.0 * ratio - factor)
        gain[2 * k] = jnp.broadcast_to(next_factor * factor, wide)
        gain[2 * k + 1] = jnp.broadcast_to(2.0 * next_factor / radius, wide)
        factor = next_factor
    gain[2 * REACH + 1] = jnp.broadcast_to(counts, wide)
    sixth = weights / 6.0

    upper_half = lax.broadcasted_iota(jnp.int32, (8, half), 0) < 4
    upper_tile = lax.broadcasted_iota(jnp.int32, (8, 128), 0) < 4
    groups = [(g, slice(8 * g, 8 * g + 8), slice(g * lons, (g + 1) * lons), False) for g in range(full)]
    if tail:
        groups.append((full, slice(8 * full, 8 * full + 8), slice(full * lons, full * lons + half), True))

    def place_of(g, tile):
        first = (tile % chunks) * width + (2 * g + tile // chunks) * 128
        return slice(first, first + 128)

    def gather(ref, row, g, is_tail):
        return jnp.concatenate(
            [ref[row, :, place_of(g, tile)] for tile in range(chunks if is_tail else tiles)], axis=1)

    for w in range(1, WINDOW - 1):
        at = 2 * me - REACH + w
        inside = jnp.where((at >= 0) & (at < nlat), 1.0, 0.0)
        line = cv[pl.ds(jnp.clip(at, 0, nlat - 1), 1), :] * inside
        for _, part, lanes, is_tail in groups:
            if is_tail:
                weight[w - 1, :, lanes] = sixth[part] * jnp.where(upper_half, line[:, :half], line[:, half:])
            else:
                weight[w - 1, :, lanes] = sixth[part] * line

    def copy(send, recv, source, row, first, size, w, target):
        lanes = pl.ds(first, size)
        return pltpu.make_async_remote_copy(
            src_ref=source.at[pl.ds(row, 1), :, lanes], dst_ref=window.at[pl.ds(w, 1), :, lanes],
            send_sem=mode_send.at[send], recv_sem=mode_recv.at[recv],
            device_id={"lat": target}, device_id_type=MESH)

    def whole(send, recv, w, target, source=own, row=inner):
        return lambda: copy(send, recv, source, row, 0, packed, w, target)

    def piece(chunk, send, recv, w, target):
        base = 9 + 7 * chunk
        return lambda: copy(base + send, base + recv, own, outer, chunk * width, width, w, target)

    inner_sends = (
        (whole(1, 1, 4 - core, me + 2), high1),
        (whole(2, 2, 12 - core, me - 2), low1),
        (whole(3, 3 + core, core, me + 4 - core), high2),
        (whole(5, 5 + core, 14 + core, me - 3 - core), low2),
        (whole(0, 0, 6 + 3 * core, sibling), always),
    )
    first_hops = (
        (whole(1, 1, 4 - core, sibling), low1),
        (whole(2, 2, 12 - core, sibling), high1),
    )
    relays = (
        (whole(7, 7, 2 + 3 * core, sibling, window, 4 - core), low1),
        (whole(8, 8, 10 + 3 * core, sibling, window, 12 - core), high1),
    )
    inner_arrivals = (
        (whole(0, 0, 9 - 3 * core, sibling), always),
        (whole(3, 3, 0, sibling), is0 & low2),
        (whole(4, 4, 1, sibling), is0 & low2),
        (whole(5, 5, 14, sibling), is1 & high2),
        (whole(6, 6, 15, sibling), is1 & high2),
        (whole(7, 7, 5 - 3 * core, sibling), low1),
        (whole(8, 8, 13 - 3 * core, sibling), high1),
    )

    def outer_sends(chunk):
        far, far_w = me - 4 + 7 * core, 15 - 13 * core
        far_on = (is1 & high2) | (is0 & low2)
        return tuple(
            entry for to in range(2) for entry in (
                (piece(chunk, 1 + to, 1 + core, 3 + 3 * core - 2 * to, me - core + 2 + to), high1),
                (piece(chunk, 3 + to, 3 + core, 11 + 3 * core - 2 * to, me - core - 2 + to), low1),
                (piece(chunk, 5 + to, 6 - core, far_w - 2 * to, far + to), far_on),
            )) + ((piece(chunk, 0, 0, 5 + 5 * core, sibling), always),)

    def outer_arrivals(chunk):
        return tuple(
            entry for by in range(2) for entry in (
                (piece(chunk, 1 + by, 1 + by, 3 + 3 * by - 2 * core, sibling), low1),
                (piece(chunk, 3 + by, 3 + by, 11 + 3 * by - 2 * core, sibling), high1),
            )) + (
                (piece(chunk, 0, 0, 10 - 5 * core, sibling), always),
                (piece(chunk, 5, 5, 2 - 2 * core, sibling), low2),
                (piece(chunk, 6, 6, 15 - 2 * core, sibling), high2),
            )

    def each(entries, action):
        for make, on in entries:
            @pl.when(on)
            def _(make=make):
                getattr(make(), action)()

    def project_tiles(row, chunk, halo_ref, ready):
        found = []
        for tile in (chunk, chunk + chunks):
            ready(tile)
            span = pl.ds(tile * 128, 128)
            forcing = ev[row, span] + nv[row, span] * halo_ref[span]
            pieces = split(forcing)
            fh[row, span], fl[row, span] = pieces
            found.append(dot3(project_sel, pieces, NT))
        for g, part, _, is_tail in groups:
            if is_tail:
                fields = ((chunk, jnp.where(upper_tile, found[0][part], found[1][part])),)
            else:
                fields = ((chunk, found[0][part]), (chunk + chunks, found[1][part]))
            for tile, field in fields:
                own[row, :, place_of(g, tile)] = field
                window[REACH + row, :, place_of(g, tile)] = field

    between.wait_recv()
    for chunk in range(chunks):
        project_tiles(inner, chunk, inner_halo, lambda tile: None)
    out[inner] = dot3((fh[inner], fl[inner]), both, NN)

    def arrive(tile):
        @pl.when(has_beyond)
        def _():
            halo(tile).wait_recv()

    for chunk in range(chunks):
        project_tiles(outer, chunk, outer_halo, arrive)
        if chunk == 0:
            each(inner_sends, "start")
        each(outer_sends(chunk), "start")
    each(first_hops, "wait_recv")
    each(relays, "start")
    out[outer] = dot3((fh[outer], fl[outer]), both, NN)
    each(inner_arrivals, "wait_recv")
    for chunk in range(chunks):
        each(outer_arrivals(chunk), "wait_recv")

    for g, part, lanes, is_tail in groups:
        lon = half if is_tail else lons

        def spread(value):
            return jnp.concatenate([value] * (lon // 128), axis=1)

        def shifted(value, by):
            moved = pltpu.roll(value, by % lon, 1)
            if not is_tail:
                return moved
            edge = lax.broadcasted_iota(jnp.int32, (8, lon), 1) == (0 if by == 1 else lon - 1)
            return jnp.where(edge, pltpu.roll(moved, 4, 0), moved)

        inverse = spread(gain[2 * REACH, part])
        limit = spread(gain[2 * REACH + 1, part])
        for w in range(WINDOW):
            field = gather(window, w, g, is_tail)
            left[w, :, :lon] = field
            dir_a[w, :, :lon] = field * inverse
        totals = [dir_a[REACH, :, :lon], dir_a[REACH + 1, :, :lon]]
        now, later = dir_a, dir_b
        for k in range(REACH):
            keep, push = spread(gain[2 * k, part]), spread(gain[2 * k + 1, part])
            for w in range(k + 1, WINDOW - 1 - k):
                here = now[w, :, :lon]
                sides = now[w - 1, :, :lon] + now[w + 1, :, :lon]
                mixed = 4.0 * here + sides
                laplace = shifted(mixed, 1) + shifted(mixed, -1) + (4.0 * sides - 20.0 * here)
                residual = left[w, :, :lon] - (here - weight[w - 1, :, lanes] * laplace)
                if k < REACH - 1:
                    left[w, :, :lon] = residual
                fresh = keep * here + push * residual
                later[w, :, :lon] = fresh
                if REACH <= w < REACH + 2:
                    totals[w - REACH] += jnp.where(k + 1 < limit, fresh, 0.0)
            now, later = later, now
        few = tuple(piece[part] for piece in restore_sel)
        for row in range(rows):
            change = totals[row] - gather(own, row, g, is_tail)
            if is_tail:
                change = jnp.concatenate(
                    [jnp.where(upper_half, change, 0.0), jnp.where(upper_half, 0.0, change)], axis=1)
            out[row] += dot3(split(change), few, TN)

    @pl.when(has_beyond)
    def _():
        for tile in range(tiles):
            halo(tile).wait_send()

    between.wait_send()
    each(inner_sends, "wait_send")
    each(relays, "wait_send")
    for chunk in range(chunks):
        each(outer_sends(chunk), "wait_send")


def solution(mesh):
    devices = mesh.shape["lat"]

    def local(state, east_wind, north_wind, coef, project, restore, stiffness, sweeps, mode_slots):
        rows, lons, levels = state.shape
        nlat = coef.shape[0]
        listed = mode_slots.shape[0] * mode_slots.shape[1] * 3 // 8
        full, rest = listed // 8, listed % 8
        tail = 1 if rest == 4 else 0
        full += 1 if rest and not tail else 0
        ranks = 8 * (full + tail)
        packed = full * lons + tail * lons // 2
        tiles = lons // 128
        copies = 9 + 7 * (tiles // 2)
        anywhere = pl.BlockSpec(memory_space=pl.ANY)
        vmem = pltpu.VMEM
        block = vmem((rows, lons, levels), f32)
        return pl.pallas_call(
            functools.partial(kernel, devices, full, tail),
            out_shape=pltpu.VMEM(state.shape, f32),
            in_specs=[anywhere] * 9,
            out_specs=pl.BlockSpec(memory_space=pltpu.VMEM),
            scratch_shapes=[
                block, block, block,
                vmem(coef.shape, f32), vmem(project.shape, f32), vmem(restore.shape, f32),
                vmem((1, levels), f32), vmem((1, levels), jnp.int32),
                vmem(mode_slots.shape[::-1], jnp.int32),
                vmem((lons, levels), f32), vmem((lons, levels), f32),
                vmem((rows, 8, packed), f32), vmem((WINDOW, 8, packed), f32),
                vmem((WINDOW, 8, lons), f32), vmem((WINDOW, 8, lons), f32), vmem((WINDOW, 8, lons), f32),
                vmem((WINDOW - 2, 8, packed), f32), vmem((2 * REACH + 2, ranks, 128), f32),
                vmem((rows, lons, levels), bf16), vmem((rows, lons, levels), bf16),
                pltpu.SemaphoreType.DMA((9,)),
                pltpu.SemaphoreType.DMA((tiles + 1,)), pltpu.SemaphoreType.DMA((tiles + 1,)),
                pltpu.SemaphoreType.DMA((copies,)), pltpu.SemaphoreType.DMA((copies,)),
            ],
            compiler_params=pltpu.CompilerParams(
                collective_id=0, has_side_effects=True, vmem_limit_bytes=VMEM_LIMIT),
        )(state, east_wind, north_wind, coef, project, restore, stiffness.reshape(1, levels),
          sweeps.reshape(1, levels), mode_slots.T)

    placed = (
        P(("parts", "lat"), None, None),
        P(("parts", "lat"), None, None),
        P(("parts", "lat"), None, None),
        P("parts", None),
        P(),
        P(),
        P(),
        P(),
        P("parts", None),
    )
    return jax.shard_map(
        local,
        mesh=mesh,
        in_specs=placed,
        out_specs=P(("parts", "lat"), None, None),
        check_vma=False,
    )
```

```python
import functools

import jax
import jax.numpy as jnp
from jax import lax
from jax.experimental import pallas as pl
from jax.experimental.pallas import tpu as pltpu
from jax.sharding import PartitionSpec as P

time_step = 0.2
diffusion = 0.05
coef_top = 2.0
sweep_limit = 8
highest = lax.Precision.HIGHEST
MESH = pl.DeviceIdType.MESH
f32 = jnp.float32
bf16 = jnp.bfloat16

REACH = sweep_limit - 1
WINDOW = 2 * REACH + 2
OFFSETS = (1, -1, 2, -2, 3, -3, 4, -4)
VMEM_LIMIT = 60 * 1024 * 1024

NN = (((1,), (0,)), ((), ()))
NT = (((1,), (1,)), ((), ()))
TN = (((0,), (0,)), ((), ()))


def split(x):
    high = x.astype(bf16)
    return high, (x - high.astype(f32)).astype(bf16)


def dot3(a, b, dims):
    (ah, al), (bh, bl) = a, b
    product = functools.partial(lax.dot_general, dimension_numbers=dims, preferred_element_type=f32)
    return product(ah, bh) + (product(ah, bl) + product(al, bh))


def kernel(devices, full, tail, state, east_wind, north_wind, coef, project, restore, stiffness, sweeps,
           mode_slots, out, sv, ev, nv, cv, pv, rv, stv, swv, msv, outer_halo, inner_halo, own, window, dir_a,
           dir_b, left, delta, weight, heavy, gain, fh, fl, load_sem, halo_send, halo_recv, mode_send, mode_recv):
    me = lax.axis_index("lat")
    rows, lons, levels = state.shape
    nlat = coef.shape[0]
    half = lons // 2
    ranks = 8 * (full + tail)
    core = lax.rem(me, 2)
    chip, chips = me // 2, devices // 2
    tiles = lons // 128
    chunks = tiles // 2
    width = (2 * full + tail) * 128
    packed = chunks * width
    inner, outer = 1 - core, core

    loads = [
        pltpu.make_async_copy(source, target, load_sem.at[i])
        for i, (source, target) in enumerate((
            (state, sv), (east_wind, ev), (north_wind, nv), (project, pv), (restore, rv),
            (mode_slots, msv), (stiffness, stv), (sweeps, swv), (coef, cv)))
    ]
    for load in loads:
        load.start()

    barrier = pltpu.get_barrier_semaphore()
    for offset in OFFSETS:
        @pl.when((me + offset >= 0) & (me + offset < devices))
        def _(offset=offset):
            pl.semaphore_signal(barrier, inc=1, device_id={"lat": me + offset}, device_id_type=MESH)
    pl.semaphore_wait(barrier, jnp.minimum(me, 4) + jnp.minimum(devices - 1 - me, 4))

    low1, low2, high1, high2 = chip >= 1, chip >= 2, chip + 1 < chips, chip + 2 < chips
    is0, is1 = core == 0, core == 1
    always = me >= 0
    sibling = me + 1 - 2 * core
    beyond = me - 1 + 2 * core
    has_beyond = (is0 & low1) | (is1 & high1)

    def halo(tile):
        span = pl.ds(tile * 128, 128)
        return pltpu.make_async_remote_copy(
            src_ref=state.at[outer, span], dst_ref=outer_halo.at[span],
            send_sem=halo_send.at[tile], recv_sem=halo_recv.at[tile],
            device_id={"lat": beyond}, device_id_type=MESH)

    between = pltpu.make_async_remote_copy(
        src_ref=state.at[inner], dst_ref=inner_halo,
        send_sem=halo_send.at[tiles], recv_sem=halo_recv.at[tiles],
        device_id={"lat": sibling}, device_id_type=MESH)

    @pl.when(has_beyond)
    def _():
        for chunk in range(chunks):
            halo(chunk).start()
            halo(chunk + chunks).start()

    between.start()

    @pl.when(jnp.logical_not(has_beyond))
    def _():
        outer_halo[...] = jnp.zeros_like(outer_halo)

    for w in range(WINDOW):
        at = 2 * me - REACH + w

        @pl.when((at < 0) | (at >= nlat))
        def _(w=w):
            window[w] = jnp.zeros(window.shape[1:], f32)

    for load in loads[:3]:
        load.wait()
    sign0 = (0.5 * time_step) * (2 * core - 1).astype(f32)
    for row, sign in ((inner, sign0), (outer, -sign0)):
        here, other = sv[row], sv[1 - row]
        east = pltpu.roll(here, lons - 1, 0)
        west = pltpu.roll(here, 1, 0)
        wind = nv[row] * sign
        ev[row] = (here - (0.5 * time_step) * ev[row] * (east - west) - wind * other
                   + (time_step * diffusion) * (east + west + other - 4.0 * here))
        nv[row] = wind + time_step * diffusion

    for load in loads[3:]:
        load.wait()
    number = lax.broadcasted_iota(jnp.int32, (levels, mode_slots.shape[1]), 0)
    hit = jnp.zeros(number.shape, f32)
    for slot in range(mode_slots.shape[0]):
        hit = jnp.maximum(hit, jnp.where(msv[slot:slot + 1, :] == number, 1.0, 0.0))
    hit = jnp.max(hit, axis=1, keepdims=True)
    listed = jnp.transpose(jnp.broadcast_to(hit, (levels, levels)))[0:1]
    before = lax.broadcasted_iota(jnp.int32, (levels, levels), 0) < lax.broadcasted_iota(
        jnp.int32, (levels, levels), 1)
    rank = lax.dot_general(
        jnp.broadcast_to(listed, (8, levels)).astype(bf16), jnp.where(before, 1.0, 0.0).astype(bf16),
        NN, preferred_element_type=f32)[0:1]
    place = lax.broadcasted_iota(jnp.int32, (ranks, levels), 0)
    place = jnp.where(place < 8 * full + 4, place, place - 4 * tail)
    chosen = jnp.where(rank == place.astype(f32), 1.0, 0.0) * listed
    used = jnp.sum(chosen, axis=1, keepdims=True)
    weights = jnp.sum(chosen * stv[...], axis=1, keepdims=True) + (1.0 - used)
    counts = jnp.sum(chosen * swv[...].astype(f32), axis=1, keepdims=True)
    project_sel = split(lax.dot_general(chosen, pv[...], NT, precision=highest, preferred_element_type=f32))
    restore_sel = split(lax.dot_general(chosen, rv[...], NN, precision=highest, preferred_element_type=f32))
    both = split(lax.dot_general(pv[...], rv[...], NN, precision=highest, preferred_element_type=f32))

    upper = 1.0 + weights * (coef_top * 16.0 / 3.0)
    centre = (upper + 1.0) * 0.5
    radius = (upper - 1.0) * 0.5
    ratio = centre / radius
    factor = 1.0 / ratio
    wide = (ranks, 128)
    gain[2 * REACH] = jnp.broadcast_to(1.0 / centre, wide)
    for k in range(REACH):
        next_factor = 1.0 / (2.0 * ratio - factor)
        gain[2 * k] = jnp.broadcast_to(next_factor * factor, wide)
        gain[2 * k + 1] = jnp.broadcast_to(2.0 * next_factor / radius, wide)
        factor = next_factor
    gain[2 * REACH + 1] = jnp.broadcast_to(counts, wide)
    sixth = weights / 6.0

    upper_half = lax.broadcasted_iota(jnp.int32, (8, half), 0) < 4
    upper_tile = lax.broadcasted_iota(jnp.int32, (8, 128), 0) < 4
    groups = [(g, slice(8 * g, 8 * g + 8), slice(g * lons, (g + 1) * lons), False) for g in range(full)]
    if tail:
        groups.append((full, slice(8 * full, 8 * full + 8), slice(full * lons, full * lons + half), True))

    def place_of(g, tile):
        first = (tile % chunks) * width + (2 * g + tile // chunks) * 128
        return slice(first, first + 128)

    def gather(ref, row, g, is_tail):
        return jnp.concatenate(
            [ref[row, :, place_of(g, tile)] for tile in range(chunks if is_tail else tiles)], axis=1)

    for w in range(1, WINDOW - 1):
        at = 2 * me - REACH + w
        inside = jnp.where((at >= 0) & (at < nlat), 1.0, 0.0)
        line = cv[pl.ds(jnp.clip(at, 0, nlat - 1), 1), :] * inside
        for _, part, lanes, is_tail in groups:
            if is_tail:
                factor = sixth[part] * jnp.where(upper_half, line[:, :half], line[:, half:])
            else:
                factor = sixth[part] * line
            weight[w - 1, :, lanes] = factor
            heavy[w - 1, :, lanes] = 1.0 + 36.0 * factor

    def copy(send, recv, source, row, first, size, w, target):
        lanes = pl.ds(first, size)
        return pltpu.make_async_remote_copy(
            src_ref=source.at[pl.ds(row, 1), :, lanes], dst_ref=window.at[pl.ds(w, 1), :, lanes],
            send_sem=mode_send.at[send], recv_sem=mode_recv.at[recv],
            device_id={"lat": target}, device_id_type=MESH)

    def whole(send, recv, w, target, source=own, row=inner):
        return lambda: copy(send, recv, source, row, 0, packed, w, target)

    def piece(chunk, send, recv, w, target):
        base = 9 + 7 * chunk
        return lambda: copy(base + send, base + recv, own, outer, chunk * width, width, w, target)

    inner_sends = (
        (whole(1, 1, 4 - core, me + 2), high1),
        (whole(2, 2, 12 - core, me - 2), low1),
        (whole(3, 3 + core, core, me + 4 - core), high2),
        (whole(5, 5 + core, 14 + core, me - 3 - core), low2),
        (whole(0, 0, 6 + 3 * core, sibling), always),
    )
    first_hops = (
        (whole(1, 1, 4 - core, sibling), low1),
        (whole(2, 2, 12 - core, sibling), high1),
    )
    relays = (
        (whole(7, 7, 2 + 3 * core, sibling, window, 4 - core), low1),
        (whole(8, 8, 10 + 3 * core, sibling, window, 12 - core), high1),
    )
    inner_arrivals = (
        (whole(0, 0, 9 - 3 * core, sibling), always),
        (whole(3, 3, 0, sibling), is0 & low2),
        (whole(4, 4, 1, sibling), is0 & low2),
        (whole(5, 5, 14, sibling), is1 & high2),
        (whole(6, 6, 15, sibling), is1 & high2),
        (whole(7, 7, 5 - 3 * core, sibling), low1),
        (whole(8, 8, 13 - 3 * core, sibling), high1),
    )

    def outer_sends(chunk):
        far, far_w = me - 4 + 7 * core, 15 - 13 * core
        far_on = (is1 & high2) | (is0 & low2)
        return tuple(
            entry for to in range(2) for entry in (
                (piece(chunk, 1 + to, 1 + core, 3 + 3 * core - 2 * to, me - core + 2 + to), high1),
                (piece(chunk, 3 + to, 3 + core, 11 + 3 * core - 2 * to, me - core - 2 + to), low1),
                (piece(chunk, 5 + to, 6 - core, far_w - 2 * to, far + to), far_on),
            )) + ((piece(chunk, 0, 0, 5 + 5 * core, sibling), always),)

    def outer_arrivals(chunk):
        return tuple(
            entry for by in range(2) for entry in (
                (piece(chunk, 1 + by, 1 + by, 3 + 3 * by - 2 * core, sibling), low1),
                (piece(chunk, 3 + by, 3 + by, 11 + 3 * by - 2 * core, sibling), high1),
            )) + (
                (piece(chunk, 0, 0, 10 - 5 * core, sibling), always),
                (piece(chunk, 5, 5, 2 - 2 * core, sibling), low2),
                (piece(chunk, 6, 6, 15 - 2 * core, sibling), high2),
            )

    def each(entries, action):
        for make, on in entries:
            @pl.when(on)
            def _(make=make):
                getattr(make(), action)()

    def project_tiles(row, chunk, halo_ref, ready):
        found = []
        for tile in (chunk, chunk + chunks):
            ready(tile)
            span = pl.ds(tile * 128, 128)
            forcing = ev[row, span] + nv[row, span] * halo_ref[span]
            pieces = split(forcing)
            fh[row, span], fl[row, span] = pieces
            found.append(dot3(project_sel, pieces, NT))
        for g, part, _, is_tail in groups:
            if is_tail:
                fields = ((chunk, jnp.where(upper_tile, found[0][part], found[1][part])),)
            else:
                fields = ((chunk, found[0][part]), (chunk + chunks, found[1][part]))
            for tile, field in fields:
                own[row, :, place_of(g, tile)] = field
                window[REACH + row, :, place_of(g, tile)] = field

    between.wait_recv()
    for chunk in range(chunks):
        project_tiles(inner, chunk, inner_halo, lambda tile: None)
    out[inner] = dot3((fh[inner], fl[inner]), both, NN)

    def arrive(tile):
        @pl.when(has_beyond)
        def _():
            halo(tile).wait_recv()

    for chunk in range(chunks):
        project_tiles(outer, chunk, outer_halo, arrive)
        if chunk == 0:
            each(inner_sends, "start")
        each(outer_sends(chunk), "start")
    each(first_hops, "wait_recv")
    each(relays, "start")
    out[outer] = dot3((fh[outer], fl[outer]), both, NN)
    each(inner_arrivals, "wait_recv")
    for chunk in range(chunks):
        each(outer_arrivals(chunk), "wait_recv")

    for g, part, lanes, is_tail in groups:
        lon = half if is_tail else lons

        def spread(value):
            return jnp.concatenate([value] * (lon // 128), axis=1)

        def shifted(value, by):
            moved = pltpu.roll(value, by % lon, 1)
            if not is_tail:
                return moved
            edge = lax.broadcasted_iota(jnp.int32, (8, lon), 1) == (0 if by == 1 else lon - 1)
            return jnp.where(edge, pltpu.roll(moved, 4, 0), moved)

        inverse = spread(gain[2 * REACH, part])
        limit = spread(gain[2 * REACH + 1, part])
        for w in range(WINDOW):
            field = gather(window, w, g, is_tail)
            left[w, :, :lon] = field
            dir_a[w, :, :lon] = field * inverse
        totals = [dir_a[REACH, :, :lon], dir_a[REACH + 1, :, :lon]]
        now, later = dir_a, dir_b
        for k in range(REACH):
            keep, push = spread(gain[2 * k, part]), spread(gain[2 * k + 1, part])
            before, here = now[k, :, :lon], now[k + 1, :, :lon]
            for w in range(k + 1, WINDOW - 1 - k):
                after = now[w + 1, :, :lon]
                mixed = 4.0 * here + (before + after)
                around = shifted(mixed, 1) + shifted(mixed, -1) + 4.0 * mixed
                residual = (left[w, :, :lon] - heavy[w - 1, :, lanes] * here) + weight[w - 1, :, lanes] * around
                if k < REACH - 1:
                    left[w, :, :lon] = residual
                fresh = keep * here + push * residual
                if k < REACH - 1:
                    later[w, :, :lon] = fresh
                if REACH <= w < REACH + 2:
                    totals[w - REACH] += jnp.where(k + 1 < limit, fresh, 0.0)
                before, here = here, after
            now, later = later, now
        for row in range(rows):
            change = totals[row] - gather(own, row, g, is_tail)
            if is_tail:
                change = jnp.concatenate(
                    [jnp.where(upper_half, change, 0.0), jnp.where(upper_half, 0.0, change)], axis=1)
            delta[row, part] = change

    few = jnp.concatenate([restore_sel[0], restore_sel[1], restore_sel[0]], axis=0)
    for row in range(rows):
        high, low = split(delta[row])
        out[row] += lax.dot_general(
            jnp.concatenate([high, high, low], axis=0), few, TN, preferred_element_type=f32)

    @pl.when(has_beyond)
    def _():
        for tile in range(tiles):
            halo(tile).wait_send()

    between.wait_send()
    each(inner_sends, "wait_send")
    each(relays, "wait_send")
    for chunk in range(chunks):
        each(outer_sends(chunk), "wait_send")


def solution(mesh):
    devices = mesh.shape["lat"]

    def local(state, east_wind, north_wind, coef, project, restore, stiffness, sweeps, mode_slots):
        rows, lons, levels = state.shape
        nlat = coef.shape[0]
        listed = mode_slots.shape[0] * mode_slots.shape[1] * 3 // 8
        full, rest = listed // 8, listed % 8
        tail = 1 if rest == 4 else 0
        full += 1 if rest and not tail else 0
        ranks = 8 * (full + tail)
        packed = full * lons + tail * lons // 2
        tiles = lons // 128
        copies = 9 + 7 * (tiles // 2)
        anywhere = pl.BlockSpec(memory_space=pl.ANY)
        vmem = pltpu.VMEM
        block = vmem((rows, lons, levels), f32)
        return pl.pallas_call(
            functools.partial(kernel, devices, full, tail),
            out_shape=pltpu.VMEM(state.shape, f32),
            in_specs=[anywhere] * 9,
            out_specs=pl.BlockSpec(memory_space=pltpu.VMEM),
            scratch_shapes=[
                block, block, block,
                vmem(coef.shape, f32), vmem(project.shape, f32), vmem(restore.shape, f32),
                vmem((1, levels), f32), vmem((1, levels), jnp.int32),
                vmem(mode_slots.shape[::-1], jnp.int32),
                vmem((lons, levels), f32), vmem((lons, levels), f32),
                vmem((rows, 8, packed), f32), vmem((WINDOW, 8, packed), f32),
                vmem((WINDOW, 8, lons), f32), vmem((WINDOW, 8, lons), f32), vmem((WINDOW, 8, lons), f32),
                vmem((rows, ranks, lons), f32), vmem((WINDOW - 2, 8, packed), f32),
                vmem((WINDOW - 2, 8, packed), f32), vmem((2 * REACH + 2, ranks, 128), f32),
                vmem((rows, lons, levels), bf16), vmem((rows, lons, levels), bf16),
                pltpu.SemaphoreType.DMA((9,)),
                pltpu.SemaphoreType.DMA((tiles + 1,)), pltpu.SemaphoreType.DMA((tiles + 1,)),
                pltpu.SemaphoreType.DMA((copies,)), pltpu.SemaphoreType.DMA((copies,)),
            ],
            compiler_params=pltpu.CompilerParams(
                collective_id=0, has_side_effects=True, vmem_limit_bytes=VMEM_LIMIT),
        )(state, east_wind, north_wind, coef, project, restore, stiffness.reshape(1, levels),
          sweeps.reshape(1, levels), mode_slots.T)

    placed = (
        P(("parts", "lat"), None, None),
        P(("parts", "lat"), None, None),
        P(("parts", "lat"), None, None),
        P("parts", None),
        P(),
        P(),
        P(),
        P(),
        P("parts", None),
    )
    return jax.shard_map(
        local,
        mesh=mesh,
        in_specs=placed,
        out_specs=P(("parts", "lat"), None, None),
        check_vma=False,
    )
```

```python
import functools

import jax
import jax.numpy as jnp
from jax import lax
from jax.experimental import pallas as pl
from jax.experimental.pallas import tpu as pltpu
from jax.sharding import PartitionSpec as P

time_step = 0.2
diffusion = 0.05
coef_top = 2.0
sweep_limit = 8
highest = lax.Precision.HIGHEST
MESH = pl.DeviceIdType.MESH
f32 = jnp.float32
bf16 = jnp.bfloat16

REACH = sweep_limit - 1
WINDOW = 2 * REACH + 2
OFFSETS = (1, -1, 2, -2, 3, -3, 4, -4)
VMEM_LIMIT = 60 * 1024 * 1024

NN = (((1,), (0,)), ((), ()))
NT = (((1,), (1,)), ((), ()))
TN = (((0,), (0,)), ((), ()))


def split(x):
    high = x.astype(bf16)
    return high, (x - high.astype(f32)).astype(bf16)


def dot3(a, b, dims):
    (ah, al), (bh, bl) = a, b
    product = functools.partial(lax.dot_general, dimension_numbers=dims, preferred_element_type=f32)
    return product(ah, bh) + (product(ah, bl) + product(al, bh))


def kernel(devices, full, tail, state, east_wind, north_wind, coef, project, restore, stiffness, sweeps,
           mode_slots, out, sv, ev, nv, cv, pv, rv, stv, swv, msv, outer_halo, inner_halo, own, window, dir_a,
           dir_b, left, delta, weight, heavy, gain, fh, fl, load_sem, halo_send, halo_recv, mode_send, mode_recv):
    me = lax.axis_index("lat")
    rows, lons, levels = state.shape
    nlat = coef.shape[0]
    half = lons // 2
    ranks = 8 * (full + tail)
    core = lax.rem(me, 2)
    chip, chips = me // 2, devices // 2
    tiles = lons // 128
    chunks = tiles // 2
    width = (2 * full + tail) * 128
    packed = chunks * width
    inner, outer = 1 - core, core

    loads = [
        pltpu.make_async_copy(source, target, load_sem.at[i])
        for i, (source, target) in enumerate((
            (state, sv), (east_wind, ev), (north_wind, nv), (project, pv), (restore, rv),
            (mode_slots, msv), (stiffness, stv), (sweeps, swv), (coef, cv)))
    ]
    for load in loads:
        load.start()

    barrier = pltpu.get_barrier_semaphore()
    for offset in OFFSETS:
        @pl.when((me + offset >= 0) & (me + offset < devices))
        def _(offset=offset):
            pl.semaphore_signal(barrier, inc=1, device_id={"lat": me + offset}, device_id_type=MESH)
    pl.semaphore_wait(barrier, jnp.minimum(me, 4) + jnp.minimum(devices - 1 - me, 4))

    low1, low2, high1, high2 = chip >= 1, chip >= 2, chip + 1 < chips, chip + 2 < chips
    is0, is1 = core == 0, core == 1
    always = me >= 0
    sibling = me + 1 - 2 * core
    beyond = me - 1 + 2 * core
    has_beyond = (is0 & low1) | (is1 & high1)

    def halo(tile):
        span = pl.ds(tile * 128, 128)
        return pltpu.make_async_remote_copy(
            src_ref=state.at[outer, span], dst_ref=outer_halo.at[span],
            send_sem=halo_send.at[tile], recv_sem=halo_recv.at[tile],
            device_id={"lat": beyond}, device_id_type=MESH)

    between = pltpu.make_async_remote_copy(
        src_ref=state.at[inner], dst_ref=inner_halo,
        send_sem=halo_send.at[tiles], recv_sem=halo_recv.at[tiles],
        device_id={"lat": sibling}, device_id_type=MESH)

    @pl.when(has_beyond)
    def _():
        for chunk in range(chunks):
            halo(chunk).start()
            halo(chunk + chunks).start()

    between.start()

    @pl.when(jnp.logical_not(has_beyond))
    def _():
        outer_halo[...] = jnp.zeros_like(outer_halo)

    for w in range(WINDOW):
        at = 2 * me - REACH + w

        @pl.when((at < 0) | (at >= nlat))
        def _(w=w):
            window[w] = jnp.zeros(window.shape[1:], f32)

    for load in loads[:3]:
        load.wait()
    sign0 = (0.5 * time_step) * (2 * core - 1).astype(f32)
    for row, sign in ((inner, sign0), (outer, -sign0)):
        here, other = sv[row], sv[1 - row]
        east = pltpu.roll(here, lons - 1, 0)
        west = pltpu.roll(here, 1, 0)
        wind = nv[row] * sign
        ev[row] = (here - (0.5 * time_step) * ev[row] * (east - west) - wind * other
                   + (time_step * diffusion) * (east + west + other - 4.0 * here))
        nv[row] = wind + time_step * diffusion

    for load in loads[3:]:
        load.wait()
    number = lax.broadcasted_iota(jnp.int32, (levels, mode_slots.shape[1]), 0)
    hit = jnp.zeros(number.shape, f32)
    for slot in range(mode_slots.shape[0]):
        hit = jnp.maximum(hit, jnp.where(msv[slot:slot + 1, :] == number, 1.0, 0.0))
    hit = jnp.max(hit, axis=1, keepdims=True)
    listed = jnp.transpose(jnp.broadcast_to(hit, (levels, levels)))[0:1]
    before = lax.broadcasted_iota(jnp.int32, (levels, levels), 0) < lax.broadcasted_iota(
        jnp.int32, (levels, levels), 1)
    rank = lax.dot_general(
        jnp.broadcast_to(listed, (8, levels)).astype(bf16), jnp.where(before, 1.0, 0.0).astype(bf16),
        NN, preferred_element_type=f32)[0:1]
    place = lax.broadcasted_iota(jnp.int32, (ranks, levels), 0)
    place = jnp.where(place < 8 * full + 4, place, place - 4 * tail)
    chosen = jnp.where(rank == place.astype(f32), 1.0, 0.0) * listed
    used = jnp.sum(chosen, axis=1, keepdims=True)
    weights = jnp.sum(chosen * stv[...], axis=1, keepdims=True) + (1.0 - used)
    counts = jnp.sum(chosen * swv[...].astype(f32), axis=1, keepdims=True)
    project_sel = split(lax.dot_general(chosen, pv[...], NT, precision=highest, preferred_element_type=f32))
    restore_sel = split(lax.dot_general(chosen, rv[...], NN, precision=highest, preferred_element_type=f32))
    both = split(lax.dot_general(pv[...], rv[...], NN, precision=highest, preferred_element_type=f32))

    upper = 1.0 + weights * (coef_top * 16.0 / 3.0)
    centre = (upper + 1.0) * 0.5
    radius = (upper - 1.0) * 0.5
    ratio = centre / radius
    factor = 1.0 / ratio
    wide = (ranks, 128)
    gain[2 * REACH] = jnp.broadcast_to(1.0 / centre, wide)
    for k in range(REACH):
        next_factor = 1.0 / (2.0 * ratio - factor)
        gain[2 * k] = jnp.broadcast_to(next_factor * factor, wide)
        gain[2 * k + 1] = jnp.broadcast_to(2.0 * next_factor / radius, wide)
        factor = next_factor
    gain[2 * REACH + 1] = jnp.broadcast_to(counts, wide)
    sixth = weights / 6.0

    upper_half = lax.broadcasted_iota(jnp.int32, (8, half), 0) < 4
    upper_tile = lax.broadcasted_iota(jnp.int32, (8, 128), 0) < 4
    groups = [(g, slice(8 * g, 8 * g + 8), slice(g * lons, (g + 1) * lons), False) for g in range(full)]
    if tail:
        groups.append((full, slice(8 * full, 8 * full + 8), slice(full * lons, full * lons + half), True))

    def place_of(g, tile):
        first = (tile % chunks) * width + (2 * g + tile // chunks) * 128
        return slice(first, first + 128)

    def gather(ref, row, g, is_tail):
        return jnp.concatenate(
            [ref[row, :, place_of(g, tile)] for tile in range(chunks if is_tail else tiles)], axis=1)

    for w in range(1, WINDOW - 1):
        at = 2 * me - REACH + w
        inside = jnp.where((at >= 0) & (at < nlat), 1.0, 0.0)
        line = cv[pl.ds(jnp.clip(at, 0, nlat - 1), 1), :] * inside
        for _, part, lanes, is_tail in groups:
            if is_tail:
                factor = sixth[part] * jnp.where(upper_half, line[:, :half], line[:, half:])
            else:
                factor = sixth[part] * line
            weight[w - 1, :, lanes] = factor
            heavy[w - 1, :, lanes] = 1.0 + 36.0 * factor

    def copy(send, recv, source, row, first, size, w, target):
        lanes = pl.ds(first, size)
        return pltpu.make_async_remote_copy(
            src_ref=source.at[pl.ds(row, 1), :, lanes], dst_ref=window.at[pl.ds(w, 1), :, lanes],
            send_sem=mode_send.at[send], recv_sem=mode_recv.at[recv],
            device_id={"lat": target}, device_id_type=MESH)

    def whole(send, recv, w, target, source=own, row=inner):
        return lambda: copy(send, recv, source, row, 0, packed, w, target)

    def piece(chunk, send, recv, w, target, source=own, row=outer):
        base = 9 + 7 * chunk
        return lambda: copy(base + send, base + recv, source, row, chunk * width, width, w, target)

    inner_sends = (
        (whole(1, 1, 4 - core, me + 2), high1),
        (whole(2, 2, 12 - core, me - 2), low1),
        (whole(3, 3 + core, core, me + 4 - core), high2),
        (whole(5, 5 + core, 14 + core, me - 3 - core), low2),
        (whole(0, 0, 6 + 3 * core, sibling), always),
    )
    first_hops = (
        (whole(1, 1, 4 - core, sibling), low1),
        (whole(2, 2, 12 - core, sibling), high1),
    )
    relays = (
        (whole(7, 7, 2 + 3 * core, sibling, window, 4 - core), low1),
        (whole(8, 8, 10 + 3 * core, sibling, window, 12 - core), high1),
    )
    inner_arrivals = (
        (whole(0, 0, 9 - 3 * core, sibling), always),
        (whole(3, 3, 0, sibling), is0 & low2),
        (whole(4, 4, 1, sibling), is0 & low2),
        (whole(5, 5, 14, sibling), is1 & high2),
        (whole(6, 6, 15, sibling), is1 & high2),
        (whole(7, 7, 5 - 3 * core, sibling), low1),
        (whole(8, 8, 13 - 3 * core, sibling), high1),
    )

    def outer_sends(chunk):
        far, far_w = me - 4 + 7 * core, 15 - 13 * core
        far_on = (is1 & high2) | (is0 & low2)
        if chunk < chunks - 1:
            return (
                (piece(chunk, 1, 1 + core, 3 + core, me + 2), high1),
                (piece(chunk, 3, 3 + core, 11 + core, me - 2), low1),
                (piece(chunk, 5, 6 - core, far_w, far), far_on),
                (piece(chunk, 6, 6 - core, far_w - 2, far + 1), far_on),
                (piece(chunk, 0, 0, 5 + 5 * core, sibling), always),
            )
        return tuple(
            entry for to in range(2) for entry in (
                (piece(chunk, 1 + to, 1 + core, 3 + 3 * core - 2 * to, me - core + 2 + to), high1),
                (piece(chunk, 3 + to, 3 + core, 11 + 3 * core - 2 * to, me - core - 2 + to), low1),
                (piece(chunk, 5 + to, 6 - core, far_w - 2 * to, far + to), far_on),
            )) + ((piece(chunk, 0, 0, 5 + 5 * core, sibling), always),)

    outer_hops = tuple(
        entry for chunk in range(chunks - 1) for entry in (
            (piece(chunk, 1, 1 + core, 3 + core, sibling), low1),
            (piece(chunk, 3, 3 + core, 11 + core, sibling), high1),
        ))
    outer_relays = tuple(
        entry for chunk in range(chunks - 1) for entry in (
            (piece(chunk, 2, 1 + core, 1 + 5 * core, sibling, window, 3 + core), low1),
            (piece(chunk, 4, 3 + core, 9 + 5 * core, sibling, window, 11 + core), high1),
        ))

    def outer_arrivals(chunk):
        if chunk < chunks - 1:
            return (
                (piece(chunk, 1, 2 - core, 6 - 5 * core, sibling), low1),
                (piece(chunk, 3, 4 - core, 14 - 5 * core, sibling), high1),
                (piece(chunk, 0, 0, 10 - 5 * core, sibling), always),
                (piece(chunk, 5, 5, 2 - 2 * core, sibling), low2),
                (piece(chunk, 6, 6, 15 - 2 * core, sibling), high2),
            )
        return tuple(
            entry for by in range(2) for entry in (
                (piece(chunk, 1 + by, 1 + by, 3 + 3 * by - 2 * core, sibling), low1),
                (piece(chunk, 3 + by, 3 + by, 11 + 3 * by - 2 * core, sibling), high1),
            )) + (
                (piece(chunk, 0, 0, 10 - 5 * core, sibling), always),
                (piece(chunk, 5, 5, 2 - 2 * core, sibling), low2),
                (piece(chunk, 6, 6, 15 - 2 * core, sibling), high2),
            )

    def each(entries, action):
        for make, on in entries:
            @pl.when(on)
            def _(make=make):
                getattr(make(), action)()

    def project_tiles(row, chunk, halo_ref, ready):
        found = []
        for tile in (chunk, chunk + chunks):
            ready(tile)
            span = pl.ds(tile * 128, 128)
            forcing = ev[row, span] + nv[row, span] * halo_ref[span]
            pieces = split(forcing)
            fh[row, span], fl[row, span] = pieces
            found.append(dot3(project_sel, pieces, NT))
        for g, part, _, is_tail in groups:
            if is_tail:
                fields = ((chunk, jnp.where(upper_tile, found[0][part], found[1][part])),)
            else:
                fields = ((chunk, found[0][part]), (chunk + chunks, found[1][part]))
            for tile, field in fields:
                own[row, :, place_of(g, tile)] = field
                window[REACH + row, :, place_of(g, tile)] = field

    between.wait_recv()
    for chunk in range(chunks):
        project_tiles(inner, chunk, inner_halo, lambda tile: None)
    out[inner] = dot3((fh[inner], fl[inner]), both, NN)

    def arrive(tile):
        @pl.when(has_beyond)
        def _():
            halo(tile).wait_recv()

    for chunk in range(chunks):
        project_tiles(outer, chunk, outer_halo, arrive)
        if chunk == 0:
            each(inner_sends, "start")
        each(outer_sends(chunk), "start")
    each(first_hops, "wait_recv")
    each(relays, "start")
    out[outer] = dot3((fh[outer], fl[outer]), both, NN)
    each(outer_hops, "wait_recv")
    each(outer_relays, "start")
    each(inner_arrivals, "wait_recv")
    for chunk in range(chunks):
        each(outer_arrivals(chunk), "wait_recv")

    for g, part, lanes, is_tail in groups:
        lon = half if is_tail else lons

        def spread(value):
            return jnp.concatenate([value] * (lon // 128), axis=1)

        def shifted(value, by):
            moved = pltpu.roll(value, by % lon, 1)
            if not is_tail:
                return moved
            edge = lax.broadcasted_iota(jnp.int32, (8, lon), 1) == (0 if by == 1 else lon - 1)
            return jnp.where(edge, pltpu.roll(moved, 4, 0), moved)

        inverse = spread(gain[2 * REACH, part])
        limit = spread(gain[2 * REACH + 1, part])
        for w in range(WINDOW):
            field = gather(window, w, g, is_tail)
            left[w, :, lanes] = field
            dir_a[w, :, lanes] = field * inverse
        totals = [dir_a[REACH, :, lanes], dir_a[REACH + 1, :, lanes]]
        now, later = dir_a, dir_b
        for k in range(REACH):
            keep, push = spread(gain[2 * k, part]), spread(gain[2 * k + 1, part])
            before, here = now[k, :, lanes], now[k + 1, :, lanes]
            for w in range(k + 1, WINDOW - 1 - k):
                after = now[w + 1, :, lanes]
                mixed = 4.0 * here + (before + after)
                around = shifted(mixed, 1) + shifted(mixed, -1) + 4.0 * mixed
                residual = (left[w, :, lanes] - heavy[w - 1, :, lanes] * here) + weight[w - 1, :, lanes] * around
                if k < REACH - 1:
                    left[w, :, lanes] = residual
                fresh = keep * here + push * residual
                if k < REACH - 1:
                    later[w, :, lanes] = fresh
                if REACH <= w < REACH + 2:
                    totals[w - REACH] += jnp.where(k + 1 < limit, fresh, 0.0)
                before, here = here, after
            now, later = later, now
        for row in range(rows):
            change = totals[row] - gather(own, row, g, is_tail)
            if is_tail:
                change = jnp.concatenate(
                    [jnp.where(upper_half, change, 0.0), jnp.where(upper_half, 0.0, change)], axis=1)
            delta[row, part] = change

    few = jnp.concatenate([restore_sel[0], restore_sel[1], restore_sel[0]], axis=0)
    for row in range(rows):
        high, low = split(delta[row])
        out[row] += lax.dot_general(
            jnp.concatenate([high, high, low], axis=0), few, TN, preferred_element_type=f32)

    @pl.when(has_beyond)
    def _():
        for tile in range(tiles):
            halo(tile).wait_send()

    between.wait_send()
    each(inner_sends, "wait_send")
    each(relays, "wait_send")
    each(outer_relays, "wait_send")
    for chunk in range(chunks):
        each(outer_sends(chunk), "wait_send")


def solution(mesh):
    devices = mesh.shape["lat"]

    def local(state, east_wind, north_wind, coef, project, restore, stiffness, sweeps, mode_slots):
        rows, lons, levels = state.shape
        nlat = coef.shape[0]
        listed = mode_slots.shape[0] * mode_slots.shape[1] * 3 // 8
        full, rest = listed // 8, listed % 8
        tail = 1 if rest == 4 else 0
        full += 1 if rest and not tail else 0
        ranks = 8 * (full + tail)
        packed = full * lons + tail * lons // 2
        tiles = lons // 128
        copies = 9 + 7 * (tiles // 2)
        anywhere = pl.BlockSpec(memory_space=pl.ANY)
        vmem = pltpu.VMEM
        block = vmem((rows, lons, levels), f32)
        return pl.pallas_call(
            functools.partial(kernel, devices, full, tail),
            out_shape=pltpu.VMEM(state.shape, f32),
            in_specs=[anywhere] * 9,
            out_specs=pl.BlockSpec(memory_space=pltpu.VMEM),
            scratch_shapes=[
                block, block, block,
                vmem(coef.shape, f32), vmem(project.shape, f32), vmem(restore.shape, f32),
                vmem((1, levels), f32), vmem((1, levels), jnp.int32),
                vmem(mode_slots.shape[::-1], jnp.int32),
                vmem((lons, levels), f32), vmem((lons, levels), f32),
                vmem((rows, 8, packed), f32), vmem((WINDOW, 8, packed), f32),
                vmem((WINDOW, 8, packed), f32), vmem((WINDOW, 8, packed), f32),
                vmem((WINDOW, 8, packed), f32),
                vmem((rows, ranks, lons), f32), vmem((WINDOW - 2, 8, packed), f32),
                vmem((WINDOW - 2, 8, packed), f32), vmem((2 * REACH + 2, ranks, 128), f32),
                vmem((rows, lons, levels), bf16), vmem((rows, lons, levels), bf16),
                pltpu.SemaphoreType.DMA((9,)),
                pltpu.SemaphoreType.DMA((tiles + 1,)), pltpu.SemaphoreType.DMA((tiles + 1,)),
                pltpu.SemaphoreType.DMA((copies,)), pltpu.SemaphoreType.DMA((copies,)),
            ],
            compiler_params=pltpu.CompilerParams(
                collective_id=0, has_side_effects=True, vmem_limit_bytes=VMEM_LIMIT),
        )(state, east_wind, north_wind, coef, project, restore, stiffness.reshape(1, levels),
          sweeps.reshape(1, levels), mode_slots.T)

    placed = (
        P(("parts", "lat"), None, None),
        P(("parts", "lat"), None, None),
        P(("parts", "lat"), None, None),
        P("parts", None),
        P(),
        P(),
        P(),
        P(),
        P("parts", None),
    )
    return jax.shard_map(
        local,
        mesh=mesh,
        in_specs=placed,
        out_specs=P(("parts", "lat"), None, None),
        check_vma=False,
    )
```

```python
import functools

import jax
import jax.numpy as jnp
from jax import lax
from jax.experimental import pallas as pl
from jax.experimental.pallas import tpu as pltpu
from jax.sharding import PartitionSpec as P

time_step = 0.2
diffusion = 0.05
coef_top = 2.0
sweep_limit = 8
highest = lax.Precision.HIGHEST
MESH = pl.DeviceIdType.MESH
f32 = jnp.float32
bf16 = jnp.bfloat16

REACH = sweep_limit - 1
WINDOW = 2 * REACH + 2
VMEM_LIMIT = 60 * 1024 * 1024

NN = (((1,), (0,)), ((), ()))
NT = (((1,), (1,)), ((), ()))
TN = (((0,), (0,)), ((), ()))


def split(x):
    high = x.astype(bf16)
    return high, (x - high.astype(f32)).astype(bf16)


def dot3(a, b, dims):
    (ah, al), (bh, bl) = a, b
    product = functools.partial(lax.dot_general, dimension_numbers=dims, preferred_element_type=f32)
    return product(ah, bh) + (product(ah, bl) + product(al, bh))


def kernel(devices, full, tail, state, east_wind, north_wind, coef, project, restore, stiffness, sweeps,
           mode_slots, out, sv, ev, nv, cv, pv, rv, stv, swv, msv, outer_halo, inner_halo, given, kept, own, window, dir_a,
           dir_b, left, delta, weight, heavy, gain, load_sem, halo_send, halo_recv, mode_send, mode_recv, knock):
    me = lax.axis_index("lat")
    rows, lons, levels = state.shape
    nlat = coef.shape[0]
    half = lons // 2
    ranks = 8 * (full + tail)
    core = lax.rem(me, 2)
    chip, chips = me // 2, devices // 2
    tiles = lons // 128
    chunks = tiles // 2
    width = (2 * full + tail) * 128
    packed = chunks * width
    inner, outer = 1 - core, core

    loads = [
        pltpu.make_async_copy(source, target, load_sem.at[i])
        for i, (source, target) in enumerate((
            (state, sv.at[pl.ds(0, rows)]), (east_wind, ev.at[pl.ds(0, rows)]), (north_wind, nv.at[pl.ds(0, rows)]),
            (project, pv), (restore, rv),
            (mode_slots, msv), (stiffness, stv), (sweeps, swv), (coef, cv)))
    ]
    for load in loads:
        load.start()

    barrier = pltpu.get_barrier_semaphore()
    low1, low2, high1, high2 = chip >= 1, chip >= 2, chip + 1 < chips, chip + 2 < chips
    is0, is1 = core == 0, core == 1
    always = me >= 0
    sibling = me + 1 - 2 * core
    beyond = me - 1 + 3 * core
    has_beyond = (is0 & low1) | (is1 & high1)

    def signal(semaphore, target, on):
        @pl.when(on)
        def _():
            pl.semaphore_signal(semaphore, inc=1, device_id={"lat": target}, device_id_type=MESH)

    def hear(semaphore, on):
        @pl.when(on)
        def _():
            pl.semaphore_wait(semaphore, 1)

    signal(barrier, sibling, always)
    signal(barrier, me - 2, is1 & low1)
    signal(barrier, me + 1, is1 & high1)
    pl.semaphore_wait(barrier, 1 + has_beyond.astype(jnp.int32))

    def halo(tile, kind=inner):
        span, slot = pl.ds(tile * 128, 128), kind * tiles + tile
        return pltpu.make_async_remote_copy(
            src_ref=state.at[outer, span], dst_ref=outer_halo.at[kind, span],
            send_sem=halo_send.at[tile], recv_sem=halo_recv.at[slot],
            device_id={"lat": beyond}, device_id_type=MESH)

    def beside(source, target, slot):
        return pltpu.make_async_remote_copy(
            src_ref=source, dst_ref=target, send_sem=halo_send.at[slot], recv_sem=halo_recv.at[slot],
            device_id={"lat": sibling}, device_id_type=MESH)

    between = beside(state.at[inner], inner_halo, 2 * tiles)
    lent = [beside(source.at[0], target.at[rows], 2 * tiles + 1 + i) for i, (source, target) in enumerate(
        ((state, sv), (east_wind, ev), (north_wind, nv)))]

    def give(tile):
        span = pl.ds(tile * 128, 128)
        return beside(given.at[0, span], given.at[0, span], 2 * tiles + 4 + tile)

    @pl.when(has_beyond)
    def _():
        for chunk in range(chunks):
            halo(chunk).start()
            halo(chunk + chunks).start()

    between.start()

    @pl.when(is0)
    def _():
        for copy in lent:
            copy.start()

    signal(knock.at[0], me + 2, is1 & high1)
    signal(knock.at[1], me - 1, is0 & low1)

    @pl.when(jnp.logical_not(low1))
    def _():
        outer_halo[0] = jnp.zeros(outer_halo.shape[1:], f32)

    @pl.when(jnp.logical_not(high1))
    def _():
        outer_halo[1] = jnp.zeros(outer_halo.shape[1:], f32)

    for w in range(WINDOW):
        at = 2 * me - REACH + w

        @pl.when((at < 0) | (at >= nlat))
        def _(w=w):
            window[w] = jnp.zeros(window.shape[1:], f32)

    for load in loads[:3]:
        load.wait()
    sign0 = (0.5 * time_step) * (2 * core - 1).astype(f32)

    def prepare(row, sign, other):
        here = sv[row]
        east = pltpu.roll(here, lons - 1, 0)
        west = pltpu.roll(here, 1, 0)
        wind = nv[row] * sign
        ev[row] = (here - (0.5 * time_step) * ev[row] * (east - west) - wind * other
                   + (time_step * diffusion) * (east + west + other - 4.0 * here))
        nv[row] = wind + time_step * diffusion

    prepare(inner, sign0, sv[outer])

    @pl.when(is1)
    def _():
        prepare(1, -sign0, sv[0])

    for load in loads[3:]:
        load.wait()
    number = lax.broadcasted_iota(jnp.int32, (levels, mode_slots.shape[1]), 0)
    hit = jnp.zeros(number.shape, f32)
    for slot in range(mode_slots.shape[0]):
        hit = jnp.maximum(hit, jnp.where(msv[slot:slot + 1, :] == number, 1.0, 0.0))
    hit = jnp.max(hit, axis=1, keepdims=True)
    listed = jnp.transpose(jnp.broadcast_to(hit, (levels, levels)))[0:1]
    before = lax.broadcasted_iota(jnp.int32, (levels, levels), 0) < lax.broadcasted_iota(
        jnp.int32, (levels, levels), 1)
    rank = lax.dot_general(
        jnp.broadcast_to(listed, (8, levels)).astype(bf16), jnp.where(before, 1.0, 0.0).astype(bf16),
        NN, preferred_element_type=f32)[0:1]
    place = lax.broadcasted_iota(jnp.int32, (ranks, levels), 0)
    place = jnp.where(place < 8 * full + 4, place, place - 4 * tail)
    chosen = jnp.where(rank == place.astype(f32), 1.0, 0.0) * listed
    used = jnp.sum(chosen, axis=1, keepdims=True)
    weights = jnp.sum(chosen * stv[...], axis=1, keepdims=True) + (1.0 - used)
    counts = jnp.sum(chosen * swv[...].astype(f32), axis=1, keepdims=True)
    project_sel = split(lax.dot_general(chosen, pv[...], NT, precision=highest, preferred_element_type=f32))
    restore_sel = split(lax.dot_general(chosen, rv[...], NN, precision=highest, preferred_element_type=f32))
    both = split(lax.dot_general(pv[...], rv[...], NN, precision=highest, preferred_element_type=f32))

    upper = 1.0 + weights * (coef_top * 16.0 / 3.0)
    centre = (upper + 1.0) * 0.5
    radius = (upper - 1.0) * 0.5
    ratio = centre / radius
    factor = 1.0 / ratio
    wide = (ranks, 128)
    gain[2 * REACH] = jnp.broadcast_to(1.0 / centre, wide)
    for k in range(REACH):
        next_factor = 1.0 / (2.0 * ratio - factor)
        gain[2 * k] = jnp.broadcast_to(next_factor * factor, wide)
        gain[2 * k + 1] = jnp.broadcast_to(2.0 * next_factor / radius, wide)
        factor = next_factor
    gain[2 * REACH + 1] = jnp.broadcast_to(counts, wide)
    sixth = weights / 6.0

    upper_half = lax.broadcasted_iota(jnp.int32, (8, half), 0) < 4
    upper_tile = lax.broadcasted_iota(jnp.int32, (8, 128), 0) < 4
    groups = [(g, slice(8 * g, 8 * g + 8), slice(g * lons, (g + 1) * lons), False) for g in range(full)]
    if tail:
        groups.append((full, slice(8 * full, 8 * full + 8), slice(full * lons, full * lons + half), True))

    def place_of(g, tile):
        first = (tile % chunks) * width + (2 * g + tile // chunks) * 128
        return slice(first, first + 128)

    def gather(ref, row, g, is_tail):
        return jnp.concatenate(
            [ref[row, :, place_of(g, tile)] for tile in range(chunks if is_tail else tiles)], axis=1)

    for w in range(1, WINDOW - 1):
        at = 2 * me - REACH + w
        inside = jnp.where((at >= 0) & (at < nlat), 1.0, 0.0)
        line = cv[pl.ds(jnp.clip(at, 0, nlat - 1), 1), :] * inside
        for _, part, lanes, is_tail in groups:
            if is_tail:
                factor = sixth[part] * jnp.where(upper_half, line[:, :half], line[:, half:])
            else:
                factor = sixth[part] * line
            weight[w - 1, :, lanes] = factor
            heavy[w - 1, :, lanes] = 1.0 + 36.0 * factor

    def copy(send, recv, source, row, first, size, w, target):
        lanes = pl.ds(first, size)
        return pltpu.make_async_remote_copy(
            src_ref=source.at[pl.ds(row, 1), :, lanes], dst_ref=window.at[pl.ds(w, 1), :, lanes],
            send_sem=mode_send.at[send], recv_sem=mode_recv.at[recv],
            device_id={"lat": target}, device_id_type=MESH)

    def whole(send, recv, w, target, source=own, row=inner):
        return lambda: copy(send, recv, source, row, 0, packed, w, target)

    def piece(chunk, send, recv, w, target, source=own, row=0):
        base = 9 + 14 * chunk
        return lambda: copy(base + send, base + recv, source, row, chunk * width, width, w, target)

    inner_sends = (
        (whole(1, 1, 4 - core, me + 2), high1),
        (whole(2, 2, 12 - core, me - 2), low1),
        (whole(3, 3 + core, core, me + 4 - core), high2),
        (whole(5, 5 + core, 14 + core, me - 3 - core), low2),
        (whole(0, 0, 6 + 3 * core, sibling), always),
    )
    first_hops = (
        (whole(1, 1, 4 - core, sibling), low1),
        (whole(2, 2, 12 - core, sibling), high1),
    )
    relays = (
        (whole(7, 7, 2 + 3 * core, sibling, window, 4 - core), low1),
        (whole(8, 8, 10 + 3 * core, sibling, window, 12 - core), high1),
    )
    inner_arrivals = (
        (whole(0, 0, 9 - 3 * core, sibling), always),
        (whole(3, 3, 0, sibling), is0 & low2),
        (whole(4, 4, 1, sibling), is0 & low2),
        (whole(5, 5, 14, sibling), is1 & high2),
        (whole(6, 6, 15, sibling), is1 & high2),
        (whole(7, 7, 5 - 3 * core, sibling), low1),
        (whole(8, 8, 13 - 3 * core, sibling), high1),
    )

    def outer_sends(chunk, kind):
        row, first, recv = 2 - kind, 7 * kind, 4 * kind
        far_on = is1 & (((kind == 0) & low2) | ((kind == 1) & high2))
        cores = range(2) if chunk == chunks - 1 else (1,)
        near = tuple(
            entry for to in cores for entry in (
                (piece(chunk, first + 3 + to, recv + 2, 11 + 3 * kind - 2 * to, me - 3 + to, own, row), is1 & low1),
                (piece(chunk, first + 1 + to, recv + 1, 3 + 3 * kind - 2 * to, me + 1 + to, own, row), is1 & high1),
            ))
        far = tuple(
            (piece(chunk, first + 5 + to, recv + 3, 15 - 13 * kind - 2 * to, me - 5 + 8 * kind + to, own, row), far_on)
            for to in range(2))
        return near + far + ((piece(chunk, first, recv, 7 + 3 * kind, sibling, own, row), is1),)

    def near_arrivals(chunk, on):
        return tuple(
            entry for kind in range(2) for entry in (
                (piece(chunk, 7 * kind + 1, 4 * kind + 1, 3 + 3 * kind - 2 * core, sibling), on & low1),
                (piece(chunk, 7 * kind + 3, 4 * kind + 2, 11 + 3 * kind - 2 * core, sibling), on & high1),
            ))

    def other_arrivals(chunk):
        return (
            (piece(chunk, 5, 3, 15 - 2 * core, sibling), high2),
            (piece(chunk, 12, 7, 2 - 2 * core, sibling), low2),
            (piece(chunk, 0, 0, 7, sibling), is0),
            (piece(chunk, 7, 4, 10, sibling), is0),
        )

    early = lax.rem(chip, 2)
    kinds = (early, 1 - early)
    outer_hops = tuple(entry for chunk in range(chunks - 1) for entry in near_arrivals(chunk, is1))
    outer_relays = tuple(
        entry for chunk in range(chunks - 1) for kind in range(2) for entry in (
            (piece(chunk, 7 * kind + 1, 4 * kind + 1, 3 + 3 * kind, sibling, window, 1 + 3 * kind), is1 & low1),
            (piece(chunk, 7 * kind + 3, 4 * kind + 2, 11 + 3 * kind, sibling, window, 9 + 3 * kind), is1 & high1),
        ))

    def each(entries, action):
        for make, on in entries:
            @pl.when(on)
            def _(make=make):
                getattr(make(), action)()

    def project_tiles(row, chunk, halo_of, ready, keep, slot, w):
        found = []
        for tile in (chunk, chunk + chunks):
            ready(tile)
            span = pl.ds(tile * 128, 128)
            forcing = ev[row, span] + nv[row, span] * halo_of(span)
            keep(tile, span, forcing)
            found.append(dot3(project_sel, split(forcing), NT))
        for g, part, _, is_tail in groups:
            if is_tail:
                fields = ((chunk, jnp.where(upper_tile, found[0][part], found[1][part])),)
            else:
                fields = ((chunk, found[0][part]), (chunk + chunks, found[1][part]))
            for tile, field in fields:
                own[slot, :, place_of(g, tile)] = field
                window[w, :, place_of(g, tile)] = field

    def keep_inner(tile, span, forcing):
        kept[span] = forcing

    between.wait_recv()
    for chunk in range(chunks):
        project_tiles(inner, chunk, lambda span: inner_halo[span], lambda tile: None, keep_inner, inner,
                      REACH + inner)
    out[inner] = dot3(split(kept[...]), both, NN)

    hear(knock.at[0], is1 & low1)
    hear(knock.at[1], is1 & high1)
    signal(knock.at[2], me + 2, is1 & high1)
    signal(knock.at[3], me - 2, is1 & low1)
    hear(knock.at[2], is1 & low1)
    hear(knock.at[3], is1 & high1)
    signal(knock.at[4], sibling, is1)
    hear(knock.at[4], is0)

    @pl.when(is0)
    def _():
        @pl.when(low1)
        def _():
            pass

        each(inner_sends, "start")
        each(first_hops, "wait_recv")
        each(relays, "start")
        for tile in range(tiles):
            give(tile).wait_recv()

    @pl.when(is1)
    def _():
        for copy in lent:
            copy.wait_recv()
        prepare(rows, 0.5 * time_step, inner_halo[...])
        for kind in kinds:
            def arrive(tile, kind=kind):
                @pl.when(((kind == 0) & low1) | ((kind == 1) & high1))
                def _():
                    halo(tile, kind).wait_recv()

            def keep(tile, span, forcing, kind=kind):
                given[kind, span] = forcing

            for chunk in range(chunks):
                project_tiles(2 - kind, chunk, lambda span, kind=kind: outer_halo[kind, span], arrive, keep,
                              2 - kind, 5 + 3 * kind)
                each(outer_sends(chunk, kind), "start")

            @pl.when(kind == 0)
            def _():
                for tile in range(tiles):
                    give(tile).start()

            if kind is kinds[0]:
                each(inner_sends, "start")
        each(first_hops, "wait_recv")
        each(relays, "start")

    out[outer] = dot3(split(given[outer]), both, NN)
    each(outer_hops, "wait_recv")
    each(outer_relays, "start")
    each(inner_arrivals, "wait_recv")
    for chunk in range(chunks):
        each(near_arrivals(chunk, always if chunk == chunks - 1 else is0), "wait_recv")
        each(other_arrivals(chunk), "wait_recv")

    for g, part, lanes, is_tail in groups:
        lon = half if is_tail else lons

        def spread(value):
            return jnp.concatenate([value] * (lon // 128), axis=1)

        def shifted(value, by):
            moved = pltpu.roll(value, by % lon, 1)
            if not is_tail:
                return moved
            edge = lax.broadcasted_iota(jnp.int32, (8, lon), 1) == (0 if by == 1 else lon - 1)
            return jnp.where(edge, pltpu.roll(moved, 4, 0), moved)

        inverse = spread(gain[2 * REACH, part])
        limit = spread(gain[2 * REACH + 1, part])
        for w in range(WINDOW):
            field = gather(window, w, g, is_tail)
            left[w, :, lanes] = field
            dir_a[w, :, lanes] = field * inverse
        totals = [dir_a[REACH, :, lanes], dir_a[REACH + 1, :, lanes]]
        now, later = dir_a, dir_b
        for k in range(REACH):
            keep, push = spread(gain[2 * k, part]), spread(gain[2 * k + 1, part])
            before, here = now[k, :, lanes], now[k + 1, :, lanes]
            for w in range(k + 1, WINDOW - 1 - k):
                after = now[w + 1, :, lanes]
                mixed = 4.0 * here + (before + after)
                around = shifted(mixed, 1) + shifted(mixed, -1) + 4.0 * mixed
                residual = (left[w, :, lanes] - heavy[w - 1, :, lanes] * here) + weight[w - 1, :, lanes] * around
                if k < REACH - 1:
                    left[w, :, lanes] = residual
                fresh = keep * here + push * residual
                if k < REACH - 1:
                    later[w, :, lanes] = fresh
                if REACH <= w < REACH + 2:
                    totals[w - REACH] += jnp.where(k + 1 < limit, fresh, 0.0)
                before, here = here, after
            now, later = later, now
        for row in range(rows):
            change = totals[row] - gather(window, REACH + row, g, is_tail)
            if is_tail:
                change = jnp.concatenate(
                    [jnp.where(upper_half, change, 0.0), jnp.where(upper_half, 0.0, change)], axis=1)
            delta[row, part] = change

    few = jnp.concatenate([restore_sel[0], restore_sel[1], restore_sel[0]], axis=0)
    for row in range(rows):
        high, low = split(delta[row])
        out[row] += lax.dot_general(
            jnp.concatenate([high, high, low], axis=0), few, TN, preferred_element_type=f32)

    @pl.when(has_beyond)
    def _():
        for chunk in range(0, chunks):
            halo(chunk).wait_send()
            halo(chunk + chunks).wait_send()

    between.wait_send()

    @pl.when(is0)
    def _():
        for copy in lent:
            copy.wait_send()

    @pl.when(is1)
    def _():
        for tile in range(tiles):
            give(tile).wait_send()

    each(inner_sends, "wait_send")
    each(relays, "wait_send")
    each(outer_relays, "wait_send")
    for kind in kinds:
        for chunk in range(chunks):
            each(outer_sends(chunk, kind), "wait_send")


def solution(mesh):
    devices = mesh.shape["lat"]

    def local(state, east_wind, north_wind, coef, project, restore, stiffness, sweeps, mode_slots):
        rows, lons, levels = state.shape
        nlat = coef.shape[0]
        listed = mode_slots.shape[0] * mode_slots.shape[1] * 3 // 8
        full, rest = listed // 8, listed % 8
        tail = 1 if rest == 4 else 0
        full += 1 if rest and not tail else 0
        ranks = 8 * (full + tail)
        packed = full * lons + tail * lons // 2
        tiles = lons // 128
        copies = 9 + 14 * (tiles // 2)
        anywhere = pl.BlockSpec(memory_space=pl.ANY)
        vmem = pltpu.VMEM
        block = vmem((rows + 1, lons, levels), f32)
        return pl.pallas_call(
            functools.partial(kernel, devices, full, tail),
            out_shape=pltpu.VMEM(state.shape, f32),
            in_specs=[anywhere] * 9,
            out_specs=pl.BlockSpec(memory_space=pltpu.VMEM),
            scratch_shapes=[
                block, block, block,
                vmem(coef.shape, f32), vmem(project.shape, f32), vmem(restore.shape, f32),
                vmem((1, levels), f32), vmem((1, levels), jnp.int32),
                vmem(mode_slots.shape[::-1], jnp.int32),
                vmem((2, lons, levels), f32), vmem((lons, levels), f32), vmem((2, lons, levels), f32),
                vmem((lons, levels), f32),
                vmem((rows + 1, 8, packed), f32), vmem((WINDOW, 8, packed), f32),
                vmem((WINDOW, 8, packed), f32), vmem((WINDOW, 8, packed), f32),
                vmem((WINDOW, 8, packed), f32),
                vmem((rows, ranks, lons), f32), vmem((WINDOW - 2, 8, packed), f32),
                vmem((WINDOW - 2, 8, packed), f32), vmem((2 * REACH + 2, ranks, 128), f32),
                pltpu.SemaphoreType.DMA((9,)),
                pltpu.SemaphoreType.DMA((3 * tiles + 4,)), pltpu.SemaphoreType.DMA((3 * tiles + 4,)),
                pltpu.SemaphoreType.DMA((copies,)), pltpu.SemaphoreType.DMA((copies,)),
                pltpu.SemaphoreType.REGULAR((5,)),
            ],
            compiler_params=pltpu.CompilerParams(
                collective_id=0, has_side_effects=True, vmem_limit_bytes=VMEM_LIMIT),
        )(state, east_wind, north_wind, coef, project, restore, stiffness.reshape(1, levels),
          sweeps.reshape(1, levels), mode_slots.T)

    placed = (
        P(("parts", "lat"), None, None),
        P(("parts", "lat"), None, None),
        P(("parts", "lat"), None, None),
        P("parts", None),
        P(),
        P(),
        P(),
        P(),
        P("parts", None),
    )
    return jax.shard_map(
        local,
        mesh=mesh,
        in_specs=placed,
        out_specs=P(("parts", "lat"), None, None),
        check_vma=False,
    )
```

```python
import functools

import jax
import jax.numpy as jnp
from jax import lax
from jax.experimental import pallas as pl
from jax.experimental.pallas import tpu as pltpu
from jax.sharding import PartitionSpec as P

time_step = 0.2
diffusion = 0.05
coef_top = 2.0
sweep_limit = 8
highest = lax.Precision.HIGHEST
MESH = pl.DeviceIdType.MESH
f32 = jnp.float32
bf16 = jnp.bfloat16

REACH = sweep_limit - 1
WINDOW = 2 * REACH + 2
VMEM_LIMIT = 60 * 1024 * 1024

NN = (((1,), (0,)), ((), ()))
NT = (((1,), (1,)), ((), ()))
TN = (((0,), (0,)), ((), ()))


def split(x):
    high = x.astype(bf16)
    return high, (x - high.astype(f32)).astype(bf16)


def dot3(a, b, dims):
    (ah, al), (bh, bl) = a, b
    product = functools.partial(lax.dot_general, dimension_numbers=dims, preferred_element_type=f32)
    return product(ah, bh) + (product(ah, bl) + product(al, bh))


def kernel(devices, full, tail, state, east_wind, north_wind, coef, project, restore, stiffness, sweeps,
           mode_slots, out, sv, ev, nv, cv, pv, rv, stv, swv, msv, outer_halo, inner_halo, given, kept, own, window, dir_a,
           dir_b, left, delta, weight, heavy, gain, load_sem, halo_send, halo_recv, mode_send, mode_recv, knock):
    me = lax.axis_index("lat")
    rows, lons, levels = state.shape
    nlat = coef.shape[0]
    half = lons // 2
    ranks = 8 * (full + tail)
    core = lax.rem(me, 2)
    chip, chips = me // 2, devices // 2
    tiles = lons // 128
    chunks = tiles // 2
    width = (2 * full + tail) * 128
    packed = chunks * width
    inner, outer = 1 - core, core

    loads = [
        pltpu.make_async_copy(source, target, load_sem.at[i])
        for i, (source, target) in enumerate((
            (state, sv.at[pl.ds(0, rows)]), (east_wind, ev.at[pl.ds(0, rows)]), (north_wind, nv.at[pl.ds(0, rows)]),
            (project, pv), (restore, rv),
            (mode_slots, msv), (stiffness, stv), (sweeps, swv), (coef, cv)))
    ]
    for load in loads:
        load.start()

    barrier = pltpu.get_barrier_semaphore()
    low1, low2, high1, high2 = chip >= 1, chip >= 2, chip + 1 < chips, chip + 2 < chips
    is0, is1 = core == 0, core == 1
    always = me >= 0
    sibling = me + 1 - 2 * core
    beyond = me - 1 + 3 * core
    has_beyond = (is0 & low1) | (is1 & high1)

    def signal(semaphore, target, on):
        @pl.when(on)
        def _():
            pl.semaphore_signal(semaphore, inc=1, device_id={"lat": target}, device_id_type=MESH)

    def hear(semaphore, on):
        @pl.when(on)
        def _():
            pl.semaphore_wait(semaphore, 1)

    signal(barrier, sibling, always)
    signal(barrier, me - 2, is1 & low1)
    signal(barrier, me + 1, is1 & high1)
    pl.semaphore_wait(barrier, 1 + has_beyond.astype(jnp.int32))

    def halo(tile, kind=inner):
        span, slot = pl.ds(tile * 128, 128), kind * tiles + tile
        return pltpu.make_async_remote_copy(
            src_ref=state.at[outer, span], dst_ref=outer_halo.at[kind, span],
            send_sem=halo_send.at[tile], recv_sem=halo_recv.at[slot],
            device_id={"lat": beyond}, device_id_type=MESH)

    def beside(source, target, slot):
        return pltpu.make_async_remote_copy(
            src_ref=source, dst_ref=target, send_sem=halo_send.at[slot], recv_sem=halo_recv.at[slot],
            device_id={"lat": sibling}, device_id_type=MESH)

    between = beside(state.at[inner], inner_halo, 2 * tiles)
    lent = [beside(source.at[0], target.at[rows], 2 * tiles + 1 + i) for i, (source, target) in enumerate(
        ((state, sv), (east_wind, ev), (north_wind, nv)))]

    def give(tile):
        span = pl.ds(tile * 128, 128)
        return beside(given.at[0, span], given.at[0, span], 2 * tiles + 4 + tile)

    held = has_beyond & (is0 & (chip == chips - 2))
    swift = has_beyond & jnp.logical_not(is0 & (chip == chips - 2))

    @pl.when(has_beyond)
    def _():
        halo(0).start()
        halo(chunks).start()

    @pl.when(swift)
    def _():
        for chunk in range(1, chunks):
            halo(chunk).start()
            halo(chunk + chunks).start()

    between.start()

    @pl.when(is0)
    def _():
        for copy in lent:
            copy.start()

    signal(knock.at[0], me + 2, is1 & high1)
    signal(knock.at[1], me - 1, is0 & low1)

    @pl.when(jnp.logical_not(low1))
    def _():
        outer_halo[0] = jnp.zeros(outer_halo.shape[1:], f32)

    @pl.when(jnp.logical_not(high1))
    def _():
        outer_halo[1] = jnp.zeros(outer_halo.shape[1:], f32)

    for w in range(WINDOW):
        at = 2 * me - REACH + w

        @pl.when((at < 0) | (at >= nlat))
        def _(w=w):
            window[w] = jnp.zeros(window.shape[1:], f32)

    for load in loads[:3]:
        load.wait()
    sign0 = (0.5 * time_step) * (2 * core - 1).astype(f32)

    def prepare(row, sign, other):
        here = sv[row]
        east = pltpu.roll(here, lons - 1, 0)
        west = pltpu.roll(here, 1, 0)
        wind = nv[row] * sign
        ev[row] = (here - (0.5 * time_step) * ev[row] * (east - west) - wind * other
                   + (time_step * diffusion) * (east + west + other - 4.0 * here))
        nv[row] = wind + time_step * diffusion

    prepare(inner, sign0, sv[outer])

    @pl.when(held)
    def _():
        halo(0).wait_send()
        halo(chunks).wait_send()
        for chunk in range(1, chunks):
            halo(chunk).start()
            halo(chunk + chunks).start()

    hear(knock.at[0], is1 & low1)
    hear(knock.at[1], is1 & high1)
    signal(knock.at[2], me + 2, is1 & high1)
    signal(knock.at[3], me - 2, is1 & low1)

    @pl.when(is1)
    def _():
        prepare(1, -sign0, sv[0])

    for load in loads[3:]:
        load.wait()
    number = lax.broadcasted_iota(jnp.int32, (levels, mode_slots.shape[1]), 0)
    hit = jnp.zeros(number.shape, f32)
    for slot in range(mode_slots.shape[0]):
        hit = jnp.maximum(hit, jnp.where(msv[slot:slot + 1, :] == number, 1.0, 0.0))
    hit = jnp.max(hit, axis=1, keepdims=True)
    listed = jnp.transpose(jnp.broadcast_to(hit, (levels, levels)))[0:1]
    before = lax.broadcasted_iota(jnp.int32, (levels, levels), 0) < lax.broadcasted_iota(
        jnp.int32, (levels, levels), 1)
    rank = lax.dot_general(
        jnp.broadcast_to(listed, (8, levels)).astype(bf16), jnp.where(before, 1.0, 0.0).astype(bf16),
        NN, preferred_element_type=f32)[0:1]
    place = lax.broadcasted_iota(jnp.int32, (ranks, levels), 0)
    place = jnp.where(place < 8 * full + 4, place, place - 4 * tail)
    chosen = jnp.where(rank == place.astype(f32), 1.0, 0.0) * listed
    used = jnp.sum(chosen, axis=1, keepdims=True)
    weights = jnp.sum(chosen * stv[...], axis=1, keepdims=True) + (1.0 - used)
    counts = jnp.sum(chosen * swv[...].astype(f32), axis=1, keepdims=True)
    project_sel = split(lax.dot_general(chosen, pv[...], NT, precision=highest, preferred_element_type=f32))
    restore_sel = split(lax.dot_general(chosen, rv[...], NN, precision=highest, preferred_element_type=f32))
    both = split(lax.dot_general(pv[...], rv[...], NN, precision=highest, preferred_element_type=f32))

    upper = 1.0 + weights * (coef_top * 16.0 / 3.0)
    centre = (upper + 1.0) * 0.5
    radius = (upper - 1.0) * 0.5
    ratio = centre / radius
    factor = 1.0 / ratio
    wide = (ranks, 128)
    gain[2 * REACH] = jnp.broadcast_to(1.0 / centre, wide)
    for k in range(REACH):
        next_factor = 1.0 / (2.0 * ratio - factor)
        gain[2 * k] = jnp.broadcast_to(next_factor * factor, wide)
        gain[2 * k + 1] = jnp.broadcast_to(2.0 * next_factor / radius, wide)
        factor = next_factor
    gain[2 * REACH + 1] = jnp.broadcast_to(counts, wide)
    sixth = weights / 6.0

    upper_half = lax.broadcasted_iota(jnp.int32, (8, half), 0) < 4
    upper_tile = lax.broadcasted_iota(jnp.int32, (8, 128), 0) < 4
    groups = [(g, slice(8 * g, 8 * g + 8), slice(g * lons, (g + 1) * lons), False) for g in range(full)]
    if tail:
        groups.append((full, slice(8 * full, 8 * full + 8), slice(full * lons, full * lons + half), True))

    def place_of(g, tile):
        first = (tile % chunks) * width + (2 * g + tile // chunks) * 128
        return slice(first, first + 128)

    def gather(ref, row, g, is_tail):
        return jnp.concatenate(
            [ref[row, :, place_of(g, tile)] for tile in range(chunks if is_tail else tiles)], axis=1)

    for w in range(1, WINDOW - 1):
        at = 2 * me - REACH + w
        inside = jnp.where((at >= 0) & (at < nlat), 1.0, 0.0)
        line = cv[pl.ds(jnp.clip(at, 0, nlat - 1), 1), :] * inside
        for _, part, lanes, is_tail in groups:
            if is_tail:
                factor = sixth[part] * jnp.where(upper_half, line[:, :half], line[:, half:])
            else:
                factor = sixth[part] * line
            weight[w - 1, :, lanes] = factor
            heavy[w - 1, :, lanes] = 1.0 + 36.0 * factor

    def copy(send, recv, source, row, first, size, w, target):
        lanes = pl.ds(first, size)
        return pltpu.make_async_remote_copy(
            src_ref=source.at[pl.ds(row, 1), :, lanes], dst_ref=window.at[pl.ds(w, 1), :, lanes],
            send_sem=mode_send.at[send], recv_sem=mode_recv.at[recv],
            device_id={"lat": target}, device_id_type=MESH)

    def whole(send, recv, w, target, source=own, row=inner):
        return lambda: copy(send, recv, source, row, 0, packed, w, target)

    def piece(chunk, send, recv, w, target, source=own, row=0):
        base = 9 + 14 * chunk
        return lambda: copy(base + send, base + recv, source, row, chunk * width, width, w, target)

    inner_sends = (
        (whole(1, 1, 4 - core, me + 2), high1),
        (whole(2, 2, 12 - core, me - 2), low1),
        (whole(3, 3 + core, core, me + 4 - core), high2),
        (whole(5, 5 + core, 14 + core, me - 3 - core), low2),
        (whole(0, 0, 6 + 3 * core, sibling), always),
    )
    first_hops = (
        (whole(1, 1, 4 - core, sibling), low1),
        (whole(2, 2, 12 - core, sibling), high1),
    )
    relays = (
        (whole(7, 7, 2 + 3 * core, sibling, window, 4 - core), low1),
        (whole(8, 8, 10 + 3 * core, sibling, window, 12 - core), high1),
    )
    inner_arrivals = (
        (whole(0, 0, 9 - 3 * core, sibling), always),
        (whole(3, 3, 0, sibling), is0 & low2),
        (whole(4, 4, 1, sibling), is0 & low2),
        (whole(5, 5, 14, sibling), is1 & high2),
        (whole(6, 6, 15, sibling), is1 & high2),
        (whole(7, 7, 5 - 3 * core, sibling), low1),
        (whole(8, 8, 13 - 3 * core, sibling), high1),
    )

    def outer_sends(chunk, kind):
        row, first, recv = 2 - kind, 7 * kind, 4 * kind
        far_on = is1 & (((kind == 0) & low2) | ((kind == 1) & high2))
        cores = range(2) if chunk == chunks - 1 else (1,)
        near = tuple(
            entry for to in cores for entry in (
                (piece(chunk, first + 3 + to, recv + 2, 11 + 3 * kind - 2 * to, me - 3 + to, own, row), is1 & low1),
                (piece(chunk, first + 1 + to, recv + 1, 3 + 3 * kind - 2 * to, me + 1 + to, own, row), is1 & high1),
            ))
        far = tuple(
            (piece(chunk, first + 5 + to, recv + 3, 15 - 13 * kind - 2 * to, me - 5 + 8 * kind + to, own, row), far_on)
            for to in range(2))
        return near + far + ((piece(chunk, first, recv, 7 + 3 * kind, sibling, own, row), is1),)

    def near_arrivals(chunk, on):
        return tuple(
            entry for kind in range(2) for entry in (
                (piece(chunk, 7 * kind + 1, 4 * kind + 1, 3 + 3 * kind - 2 * core, sibling), on & low1),
                (piece(chunk, 7 * kind + 3, 4 * kind + 2, 11 + 3 * kind - 2 * core, sibling), on & high1),
            ))

    def other_arrivals(chunk):
        return (
            (piece(chunk, 5, 3, 15 - 2 * core, sibling), high2),
            (piece(chunk, 12, 7, 2 - 2 * core, sibling), low2),
            (piece(chunk, 0, 0, 7, sibling), is0),
            (piece(chunk, 7, 4, 10, sibling), is0),
        )

    early = lax.rem(chip, 2)
    kinds = (early, 1 - early)
    outer_hops = tuple(entry for chunk in range(chunks - 1) for entry in near_arrivals(chunk, is1))
    outer_relays = tuple(
        entry for chunk in range(chunks - 1) for kind in range(2) for entry in (
            (piece(chunk, 7 * kind + 1, 4 * kind + 1, 3 + 3 * kind, sibling, window, 1 + 3 * kind), is1 & low1),
            (piece(chunk, 7 * kind + 3, 4 * kind + 2, 11 + 3 * kind, sibling, window, 9 + 3 * kind), is1 & high1),
        ))

    def each(entries, action):
        for make, on in entries:
            @pl.when(on)
            def _(make=make):
                getattr(make(), action)()

    def project_tiles(row, chunk, halo_of, ready, keep, slot, w):
        found = []
        for tile in (chunk, chunk + chunks):
            ready(tile)
            span = pl.ds(tile * 128, 128)
            forcing = ev[row, span] + nv[row, span] * halo_of(span)
            keep(tile, span, forcing)
            found.append(dot3(project_sel, split(forcing), NT))
        for g, part, _, is_tail in groups:
            if is_tail:
                fields = ((chunk, jnp.where(upper_tile, found[0][part], found[1][part])),)
            else:
                fields = ((chunk, found[0][part]), (chunk + chunks, found[1][part]))
            for tile, field in fields:
                own[slot, :, place_of(g, tile)] = field
                window[w, :, place_of(g, tile)] = field

    def keep_inner(tile, span, forcing):
        kept[span] = forcing

    between.wait_recv()
    for chunk in range(chunks):
        project_tiles(inner, chunk, lambda span: inner_halo[span], lambda tile: None, keep_inner, inner,
                      REACH + inner)
    out[inner] = dot3(split(kept[...]), both, NN)

    hear(knock.at[2], is1 & low1)
    hear(knock.at[3], is1 & high1)
    signal(knock.at[4], sibling, is1)
    hear(knock.at[4], is0)

    @pl.when(is0)
    def _():
        @pl.when(low1)
        def _():
            pass

        each(inner_sends, "start")
        each(first_hops, "wait_recv")
        each(relays, "start")
        for tile in range(tiles):
            give(tile).wait_recv()

    @pl.when(is1)
    def _():
        for copy in lent:
            copy.wait_recv()
        prepare(rows, 0.5 * time_step, inner_halo[...])
        for kind in kinds:
            def arrive(tile, kind=kind):
                @pl.when(((kind == 0) & low1) | ((kind == 1) & high1))
                def _():
                    halo(tile, kind).wait_recv()

            def keep(tile, span, forcing, kind=kind):
                given[kind, span] = forcing

            for chunk in range(chunks):
                project_tiles(2 - kind, chunk, lambda span, kind=kind: outer_halo[kind, span], arrive, keep,
                              2 - kind, 5 + 3 * kind)
                each(outer_sends(chunk, kind), "start")

            @pl.when(kind == 0)
            def _():
                for tile in range(tiles):
                    give(tile).start()

            if kind is kinds[0]:
                each(inner_sends, "start")
        each(first_hops, "wait_recv")
        each(relays, "start")

    out[outer] = dot3(split(given[outer]), both, NN)
    each(outer_hops, "wait_recv")
    each(outer_relays, "start")
    each(inner_arrivals, "wait_recv")
    for chunk in range(chunks):
        each(near_arrivals(chunk, always if chunk == chunks - 1 else is0), "wait_recv")
        each(other_arrivals(chunk), "wait_recv")

    for g, part, lanes, is_tail in groups:
        lon = half if is_tail else lons

        def spread(value):
            return jnp.concatenate([value] * (lon // 128), axis=1)

        def shifted(value, by):
            moved = pltpu.roll(value, by % lon, 1)
            if not is_tail:
                return moved
            edge = lax.broadcasted_iota(jnp.int32, (8, lon), 1) == (0 if by == 1 else lon - 1)
            return jnp.where(edge, pltpu.roll(moved, 4, 0), moved)

        inverse = spread(gain[2 * REACH, part])
        limit = spread(gain[2 * REACH + 1, part])
        for w in range(WINDOW):
            field = gather(window, w, g, is_tail)
            left[w, :, lanes] = field
            dir_a[w, :, lanes] = field * inverse
        totals = [dir_a[REACH, :, lanes], dir_a[REACH + 1, :, lanes]]
        now, later = dir_a, dir_b
        for k in range(REACH):
            keep, push = spread(gain[2 * k, part]), spread(gain[2 * k + 1, part])
            before, here = now[k, :, lanes], now[k + 1, :, lanes]
            for w in range(k + 1, WINDOW - 1 - k):
                after = now[w + 1, :, lanes]
                mixed = 4.0 * here + (before + after)
                around = shifted(mixed, 1) + shifted(mixed, -1) + 4.0 * mixed
                residual = (left[w, :, lanes] - heavy[w - 1, :, lanes] * here) + weight[w - 1, :, lanes] * around
                if k < REACH - 1:
                    left[w, :, lanes] = residual
                fresh = keep * here + push * residual
                if k < REACH - 1:
                    later[w, :, lanes] = fresh
                if REACH <= w < REACH + 2:
                    totals[w - REACH] += jnp.where(k + 1 < limit, fresh, 0.0)
                before, here = here, after
            now, later = later, now
        for row in range(rows):
            change = totals[row] - gather(window, REACH + row, g, is_tail)
            if is_tail:
                change = jnp.concatenate(
                    [jnp.where(upper_half, change, 0.0), jnp.where(upper_half, 0.0, change)], axis=1)
            delta[row, part] = change

    few = jnp.concatenate([restore_sel[0], restore_sel[1], restore_sel[0]], axis=0)
    for row in range(rows):
        high, low = split(delta[row])
        out[row] += lax.dot_general(
            jnp.concatenate([high, high, low], axis=0), few, TN, preferred_element_type=f32)

    @pl.when(swift)
    def _():
        halo(0).wait_send()
        halo(chunks).wait_send()

    @pl.when(has_beyond)
    def _():
        for chunk in range(1, chunks):
            halo(chunk).wait_send()
            halo(chunk + chunks).wait_send()

    between.wait_send()

    @pl.when(is0)
    def _():
        for copy in lent:
            copy.wait_send()

    @pl.when(is1)
    def _():
        for tile in range(tiles):
            give(tile).wait_send()

    each(inner_sends, "wait_send")
    each(relays, "wait_send")
    each(outer_relays, "wait_send")
    for kind in kinds:
        for chunk in range(chunks):
            each(outer_sends(chunk, kind), "wait_send")


def solution(mesh):
    devices = mesh.shape["lat"]

    def local(state, east_wind, north_wind, coef, project, restore, stiffness, sweeps, mode_slots):
        rows, lons, levels = state.shape
        nlat = coef.shape[0]
        listed = mode_slots.shape[0] * mode_slots.shape[1] * 3 // 8
        full, rest = listed // 8, listed % 8
        tail = 1 if rest == 4 else 0
        full += 1 if rest and not tail else 0
        ranks = 8 * (full + tail)
        packed = full * lons + tail * lons // 2
        tiles = lons // 128
        copies = 9 + 14 * (tiles // 2)
        anywhere = pl.BlockSpec(memory_space=pl.ANY)
        vmem = pltpu.VMEM
        block = vmem((rows + 1, lons, levels), f32)
        return pl.pallas_call(
            functools.partial(kernel, devices, full, tail),
            out_shape=pltpu.VMEM(state.shape, f32),
            in_specs=[anywhere] * 9,
            out_specs=pl.BlockSpec(memory_space=pltpu.VMEM),
            scratch_shapes=[
                block, block, block,
                vmem(coef.shape, f32), vmem(project.shape, f32), vmem(restore.shape, f32),
                vmem((1, levels), f32), vmem((1, levels), jnp.int32),
                vmem(mode_slots.shape[::-1], jnp.int32),
                vmem((2, lons, levels), f32), vmem((lons, levels), f32), vmem((2, lons, levels), f32),
                vmem((lons, levels), f32),
                vmem((rows + 1, 8, packed), f32), vmem((WINDOW, 8, packed), f32),
                vmem((WINDOW, 8, packed), f32), vmem((WINDOW, 8, packed), f32),
                vmem((WINDOW, 8, packed), f32),
                vmem((rows, ranks, lons), f32), vmem((WINDOW - 2, 8, packed), f32),
                vmem((WINDOW - 2, 8, packed), f32), vmem((2 * REACH + 2, ranks, 128), f32),
                pltpu.SemaphoreType.DMA((9,)),
                pltpu.SemaphoreType.DMA((3 * tiles + 4,)), pltpu.SemaphoreType.DMA((3 * tiles + 4,)),
                pltpu.SemaphoreType.DMA((copies,)), pltpu.SemaphoreType.DMA((copies,)),
                pltpu.SemaphoreType.REGULAR((5,)),
            ],
            compiler_params=pltpu.CompilerParams(
                collective_id=0, has_side_effects=True, vmem_limit_bytes=VMEM_LIMIT),
        )(state, east_wind, north_wind, coef, project, restore, stiffness.reshape(1, levels),
          sweeps.reshape(1, levels), mode_slots.T)

    placed = (
        P(("parts", "lat"), None, None),
        P(("parts", "lat"), None, None),
        P(("parts", "lat"), None, None),
        P("parts", None),
        P(),
        P(),
        P(),
        P(),
        P("parts", None),
    )
    return jax.shard_map(
        local,
        mesh=mesh,
        in_specs=placed,
        out_specs=P(("parts", "lat"), None, None),
        check_vma=False,
    )
```

```python
import functools

import jax
import jax.numpy as jnp
from jax import lax
from jax.experimental import pallas as pl
from jax.experimental.pallas import tpu as pltpu
from jax.sharding import PartitionSpec as P

time_step = 0.2
diffusion = 0.05
coef_top = 2.0
sweep_limit = 8
highest = lax.Precision.HIGHEST
MESH = pl.DeviceIdType.MESH
f32 = jnp.float32
bf16 = jnp.bfloat16

REACH = sweep_limit - 1
WINDOW = 2 * REACH + 2
VMEM_LIMIT = 60 * 1024 * 1024

NN = (((1,), (0,)), ((), ()))
NT = (((1,), (1,)), ((), ()))
TN = (((0,), (0,)), ((), ()))


def split(x):
    high = x.astype(bf16)
    return high, (x - high.astype(f32)).astype(bf16)


def dot3(a, b, dims):
    (ah, al), (bh, bl) = a, b
    product = functools.partial(lax.dot_general, dimension_numbers=dims, preferred_element_type=f32)
    return product(ah, bh) + (product(ah, bl) + product(al, bh))


def kernel(devices, full, tail, state, east_wind, north_wind, coef, project, restore, stiffness, sweeps,
           mode_slots, out, sv, ev, nv, cv, pv, rv, stv, swv, msv, outer_halo, inner_halo, given, kept, own, window, dir_a,
           dir_b, left, delta, weight, heavy, gain, load_sem, halo_send, halo_recv, mode_send, mode_recv, knock):
    me = lax.axis_index("lat")
    rows, lons, levels = state.shape
    nlat = coef.shape[0]
    half = lons // 2
    ranks = 8 * (full + tail)
    core = lax.rem(me, 2)
    chip, chips = me // 2, devices // 2
    tiles = lons // 128
    chunks = tiles // 2
    width = (2 * full + tail) * 128
    packed = chunks * width
    inner, outer = 1 - core, core

    loads = [
        pltpu.make_async_copy(source, target, load_sem.at[i])
        for i, (source, target) in enumerate((
            (state, sv.at[pl.ds(0, rows)]), (east_wind, ev.at[pl.ds(0, rows)]), (north_wind, nv.at[pl.ds(0, rows)]),
            (project, pv), (restore, rv),
            (mode_slots, msv), (stiffness, stv), (sweeps, swv), (coef, cv)))
    ]
    for load in loads:
        load.start()

    barrier = pltpu.get_barrier_semaphore()
    low1, low2, high1, high2 = chip >= 1, chip >= 2, chip + 1 < chips, chip + 2 < chips
    is0, is1 = core == 0, core == 1
    always = me >= 0
    sibling = me + 1 - 2 * core
    beyond = me - 1 + 3 * core
    has_beyond = (is0 & low1) | (is1 & high1)

    def signal(semaphore, target, on):
        @pl.when(on)
        def _():
            pl.semaphore_signal(semaphore, inc=1, device_id={"lat": target}, device_id_type=MESH)

    def hear(semaphore, on):
        @pl.when(on)
        def _():
            pl.semaphore_wait(semaphore, 1)

    signal(barrier, sibling, always)
    signal(barrier, me - 2, is1 & low1)
    signal(barrier, me + 1, is1 & high1)
    pl.semaphore_wait(barrier, 1 + has_beyond.astype(jnp.int32))

    def halo(tile, kind=inner):
        span, slot = pl.ds(tile * 128, 128), kind * tiles + tile
        return pltpu.make_async_remote_copy(
            src_ref=state.at[outer, span], dst_ref=outer_halo.at[kind, span],
            send_sem=halo_send.at[tile], recv_sem=halo_recv.at[slot],
            device_id={"lat": beyond}, device_id_type=MESH)

    def beside(source, target, slot):
        return pltpu.make_async_remote_copy(
            src_ref=source, dst_ref=target, send_sem=halo_send.at[slot], recv_sem=halo_recv.at[slot],
            device_id={"lat": sibling}, device_id_type=MESH)

    between = beside(state.at[inner], inner_halo, 2 * tiles)
    lent = [beside(source.at[0], target.at[rows], 2 * tiles + 1 + i) for i, (source, target) in enumerate(
        ((state, sv), (east_wind, ev), (north_wind, nv)))]

    def give(tile):
        span = pl.ds(tile * 128, 128)
        return beside(given.at[0, span], given.at[0, span], 2 * tiles + 4 + tile)

    held = has_beyond & ((is1 & (lax.rem(chip, 2) == 1)) | (is0 & (chip == chips - 2)))
    swift = has_beyond & jnp.logical_not((is1 & (lax.rem(chip, 2) == 1)) | (is0 & (chip == chips - 2)))

    @pl.when(has_beyond)
    def _():
        halo(0).start()
        halo(chunks).start()

    @pl.when(swift)
    def _():
        for chunk in range(1, chunks):
            halo(chunk).start()
            halo(chunk + chunks).start()

    between.start()

    @pl.when(is0)
    def _():
        for copy in lent:
            copy.start()

    signal(knock.at[0], me + 2, is1 & high1)
    signal(knock.at[1], me - 1, is0 & low1)

    @pl.when(jnp.logical_not(low1))
    def _():
        outer_halo[0] = jnp.zeros(outer_halo.shape[1:], f32)

    @pl.when(jnp.logical_not(high1))
    def _():
        outer_halo[1] = jnp.zeros(outer_halo.shape[1:], f32)

    for w in range(WINDOW):
        at = 2 * me - REACH + w

        @pl.when((at < 0) | (at >= nlat))
        def _(w=w):
            window[w] = jnp.zeros(window.shape[1:], f32)

    for load in loads[:3]:
        load.wait()
    sign0 = (0.5 * time_step) * (2 * core - 1).astype(f32)

    def prepare(row, sign, other):
        here = sv[row]
        east = pltpu.roll(here, lons - 1, 0)
        west = pltpu.roll(here, 1, 0)
        wind = nv[row] * sign
        ev[row] = (here - (0.5 * time_step) * ev[row] * (east - west) - wind * other
                   + (time_step * diffusion) * (east + west + other - 4.0 * here))
        nv[row] = wind + time_step * diffusion

    prepare(inner, sign0, sv[outer])

    @pl.when(held)
    def _():
        halo(0).wait_send()
        halo(chunks).wait_send()
        for chunk in range(1, chunks):
            halo(chunk).start()
            halo(chunk + chunks).start()

    hear(knock.at[0], is1 & low1)
    hear(knock.at[1], is1 & high1)
    signal(knock.at[2], me + 2, is1 & high1)
    signal(knock.at[3], me - 2, is1 & low1)

    @pl.when(is1)
    def _():
        prepare(1, -sign0, sv[0])

    for load in loads[3:]:
        load.wait()
    number = lax.broadcasted_iota(jnp.int32, (levels, mode_slots.shape[1]), 0)
    hit = jnp.zeros(number.shape, f32)
    for slot in range(mode_slots.shape[0]):
        hit = jnp.maximum(hit, jnp.where(msv[slot:slot + 1, :] == number, 1.0, 0.0))
    hit = jnp.max(hit, axis=1, keepdims=True)
    listed = jnp.transpose(jnp.broadcast_to(hit, (levels, levels)))[0:1]
    before = lax.broadcasted_iota(jnp.int32, (levels, levels), 0) < lax.broadcasted_iota(
        jnp.int32, (levels, levels), 1)
    rank = lax.dot_general(
        jnp.broadcast_to(listed, (8, levels)).astype(bf16), jnp.where(before, 1.0, 0.0).astype(bf16),
        NN, preferred_element_type=f32)[0:1]
    place = lax.broadcasted_iota(jnp.int32, (ranks, levels), 0)
    place = jnp.where(place < 8 * full + 4, place, place - 4 * tail)
    chosen = jnp.where(rank == place.astype(f32), 1.0, 0.0) * listed
    used = jnp.sum(chosen, axis=1, keepdims=True)
    weights = jnp.sum(chosen * stv[...], axis=1, keepdims=True) + (1.0 - used)
    counts = jnp.sum(chosen * swv[...].astype(f32), axis=1, keepdims=True)
    project_sel = split(lax.dot_general(chosen, pv[...], NT, precision=highest, preferred_element_type=f32))
    restore_sel = split(lax.dot_general(chosen, rv[...], NN, precision=highest, preferred_element_type=f32))
    both = split(lax.dot_general(pv[...], rv[...], NN, precision=highest, preferred_element_type=f32))

    upper = 1.0 + weights * (coef_top * 16.0 / 3.0)
    centre = (upper + 1.0) * 0.5
    radius = (upper - 1.0) * 0.5
    ratio = centre / radius
    factor = 1.0 / ratio
    wide = (ranks, 128)
    gain[2 * REACH] = jnp.broadcast_to(1.0 / centre, wide)
    for k in range(REACH):
        next_factor = 1.0 / (2.0 * ratio - factor)
        gain[2 * k] = jnp.broadcast_to(next_factor * factor, wide)
        gain[2 * k + 1] = jnp.broadcast_to(2.0 * next_factor / radius, wide)
        factor = next_factor
    gain[2 * REACH + 1] = jnp.broadcast_to(counts, wide)
    sixth = weights / 6.0

    upper_half = lax.broadcasted_iota(jnp.int32, (8, half), 0) < 4
    upper_tile = lax.broadcasted_iota(jnp.int32, (8, 128), 0) < 4
    groups = [(g, slice(8 * g, 8 * g + 8), slice(g * lons, (g + 1) * lons), False) for g in range(full)]
    if tail:
        groups.append((full, slice(8 * full, 8 * full + 8), slice(full * lons, full * lons + half), True))

    def place_of(g, tile):
        first = (tile % chunks) * width + (2 * g + tile // chunks) * 128
        return slice(first, first + 128)

    def gather(ref, row, g, is_tail):
        return jnp.concatenate(
            [ref[row, :, place_of(g, tile)] for tile in range(chunks if is_tail else tiles)], axis=1)

    for w in range(1, WINDOW - 1):
        at = 2 * me - REACH + w
        inside = jnp.where((at >= 0) & (at < nlat), 1.0, 0.0)
        line = cv[pl.ds(jnp.clip(at, 0, nlat - 1), 1), :] * inside
        for _, part, lanes, is_tail in groups:
            if is_tail:
                factor = sixth[part] * jnp.where(upper_half, line[:, :half], line[:, half:])
            else:
                factor = sixth[part] * line
            weight[w - 1, :, lanes] = factor
            heavy[w - 1, :, lanes] = 1.0 + 36.0 * factor

    def copy(send, recv, source, row, first, size, w, target):
        lanes = pl.ds(first, size)
        return pltpu.make_async_remote_copy(
            src_ref=source.at[pl.ds(row, 1), :, lanes], dst_ref=window.at[pl.ds(w, 1), :, lanes],
            send_sem=mode_send.at[send], recv_sem=mode_recv.at[recv],
            device_id={"lat": target}, device_id_type=MESH)

    def whole(send, recv, w, target, source=own, row=inner):
        return lambda: copy(send, recv, source, row, 0, packed, w, target)

    def piece(chunk, send, recv, w, target, source=own, row=0):
        base = 9 + 14 * chunk
        return lambda: copy(base + send, base + recv, source, row, chunk * width, width, w, target)

    inner_sends = (
        (whole(1, 1, 4 - core, me + 2), high1),
        (whole(2, 2, 12 - core, me - 2), low1),
        (whole(3, 3 + core, core, me + 4 - core), high2),
        (whole(5, 5 + core, 14 + core, me - 3 - core), low2),
        (whole(0, 0, 6 + 3 * core, sibling), always),
    )
    first_hops = (
        (whole(1, 1, 4 - core, sibling), low1),
        (whole(2, 2, 12 - core, sibling), high1),
    )
    relays = (
        (whole(7, 7, 2 + 3 * core, sibling, window, 4 - core), low1),
        (whole(8, 8, 10 + 3 * core, sibling, window, 12 - core), high1),
    )
    inner_arrivals = (
        (whole(0, 0, 9 - 3 * core, sibling), always),
        (whole(3, 3, 0, sibling), is0 & low2),
        (whole(4, 4, 1, sibling), is0 & low2),
        (whole(5, 5, 14, sibling), is1 & high2),
        (whole(6, 6, 15, sibling), is1 & high2),
        (whole(7, 7, 5 - 3 * core, sibling), low1),
        (whole(8, 8, 13 - 3 * core, sibling), high1),
    )

    def outer_sends(chunk, kind):
        row, first, recv = 2 - kind, 7 * kind, 4 * kind
        far_on = is1 & (((kind == 0) & low2) | ((kind == 1) & high2))
        cores = range(2) if chunk == chunks - 1 else (1,)
        near = tuple(
            entry for to in cores for entry in (
                (piece(chunk, first + 3 + to, recv + 2, 11 + 3 * kind - 2 * to, me - 3 + to, own, row), is1 & low1),
                (piece(chunk, first + 1 + to, recv + 1, 3 + 3 * kind - 2 * to, me + 1 + to, own, row), is1 & high1),
            ))
        far = tuple(
            (piece(chunk, first + 5 + to, recv + 3, 15 - 13 * kind - 2 * to, me - 5 + 8 * kind + to, own, row), far_on)
            for to in range(2))
        return near + far + ((piece(chunk, first, recv, 7 + 3 * kind, sibling, own, row), is1),)

    def near_arrivals(chunk, on):
        return tuple(
            entry for kind in range(2) for entry in (
                (piece(chunk, 7 * kind + 1, 4 * kind + 1, 3 + 3 * kind - 2 * core, sibling), on & low1),
                (piece(chunk, 7 * kind + 3, 4 * kind + 2, 11 + 3 * kind - 2 * core, sibling), on & high1),
            ))

    def other_arrivals(chunk):
        return (
            (piece(chunk, 5, 3, 15 - 2 * core, sibling), high2),
            (piece(chunk, 12, 7, 2 - 2 * core, sibling), low2),
            (piece(chunk, 0, 0, 7, sibling), is0),
            (piece(chunk, 7, 4, 10, sibling), is0),
        )

    early = lax.rem(chip, 2)
    kinds = (early, 1 - early)
    outer_hops = tuple(entry for chunk in range(chunks - 1) for entry in near_arrivals(chunk, is1))
    outer_relays = tuple(
        entry for chunk in range(chunks - 1) for kind in range(2) for entry in (
            (piece(chunk, 7 * kind + 1, 4 * kind + 1, 3 + 3 * kind, sibling, window, 1 + 3 * kind), is1 & low1),
            (piece(chunk, 7 * kind + 3, 4 * kind + 2, 11 + 3 * kind, sibling, window, 9 + 3 * kind), is1 & high1),
        ))

    def each(entries, action):
        for make, on in entries:
            @pl.when(on)
            def _(make=make):
                getattr(make(), action)()

    def project_tiles(row, chunk, halo_of, ready, keep, slot, w):
        found = []
        for tile in (chunk, chunk + chunks):
            ready(tile)
            span = pl.ds(tile * 128, 128)
            forcing = ev[row, span] + nv[row, span] * halo_of(span)
            keep(tile, span, forcing)
            found.append(dot3(project_sel, split(forcing), NT))
        for g, part, _, is_tail in groups:
            if is_tail:
                fields = ((chunk, jnp.where(upper_tile, found[0][part], found[1][part])),)
            else:
                fields = ((chunk, found[0][part]), (chunk + chunks, found[1][part]))
            for tile, field in fields:
                own[slot, :, place_of(g, tile)] = field
                window[w, :, place_of(g, tile)] = field

    def keep_inner(tile, span, forcing):
        kept[span] = forcing

    between.wait_recv()
    for chunk in range(chunks):
        project_tiles(inner, chunk, lambda span: inner_halo[span], lambda tile: None, keep_inner, inner,
                      REACH + inner)
    out[inner] = dot3(split(kept[...]), both, NN)

    hear(knock.at[2], is1 & low1)
    hear(knock.at[3], is1 & high1)
    signal(knock.at[4], sibling, is1)
    hear(knock.at[4], is0)

    @pl.when(is0)
    def _():
        @pl.when(low1)
        def _():
            pass

        each(inner_sends, "start")
        each(first_hops, "wait_recv")
        each(relays, "start")
        for tile in range(tiles):
            give(tile).wait_recv()

    @pl.when(is1)
    def _():
        for copy in lent:
            copy.wait_recv()
        prepare(rows, 0.5 * time_step, inner_halo[...])
        for kind in kinds:
            def arrive(tile, kind=kind):
                @pl.when(((kind == 0) & low1) | ((kind == 1) & high1))
                def _():
                    halo(tile, kind).wait_recv()

            def keep(tile, span, forcing, kind=kind):
                given[kind, span] = forcing

            for chunk in range(chunks):
                project_tiles(2 - kind, chunk, lambda span, kind=kind: outer_halo[kind, span], arrive, keep,
                              2 - kind, 5 + 3 * kind)
                each(outer_sends(chunk, kind), "start")

            @pl.when(kind == 0)
            def _():
                for tile in range(tiles):
                    give(tile).start()

            if kind is kinds[0]:
                each(inner_sends, "start")
        each(first_hops, "wait_recv")
        each(relays, "start")

    out[outer] = dot3(split(given[outer]), both, NN)
    each(outer_hops, "wait_recv")
    each(outer_relays, "start")
    each(inner_arrivals, "wait_recv")
    for chunk in range(chunks):
        each(near_arrivals(chunk, always if chunk == chunks - 1 else is0), "wait_recv")
        each(other_arrivals(chunk), "wait_recv")

    for g, part, lanes, is_tail in groups:
        lon = half if is_tail else lons

        def spread(value):
            return jnp.concatenate([value] * (lon // 128), axis=1)

        def shifted(value, by):
            moved = pltpu.roll(value, by % lon, 1)
            if not is_tail:
                return moved
            edge = lax.broadcasted_iota(jnp.int32, (8, lon), 1) == (0 if by == 1 else lon - 1)
            return jnp.where(edge, pltpu.roll(moved, 4, 0), moved)

        inverse = spread(gain[2 * REACH, part])
        limit = spread(gain[2 * REACH + 1, part])
        for w in range(WINDOW):
            field = gather(window, w, g, is_tail)
            left[w, :, lanes] = field
            dir_a[w, :, lanes] = field * inverse
        totals = [dir_a[REACH, :, lanes], dir_a[REACH + 1, :, lanes]]
        now, later = dir_a, dir_b
        for k in range(REACH):
            keep, push = spread(gain[2 * k, part]), spread(gain[2 * k + 1, part])
            before, here = now[k, :, lanes], now[k + 1, :, lanes]
            for w in range(k + 1, WINDOW - 1 - k):
                after = now[w + 1, :, lanes]
                mixed = 4.0 * here + (before + after)
                around = shifted(mixed, 1) + shifted(mixed, -1) + 4.0 * mixed
                residual = (left[w, :, lanes] - heavy[w - 1, :, lanes] * here) + weight[w - 1, :, lanes] * around
                if k < REACH - 1:
                    left[w, :, lanes] = residual
                fresh = keep * here + push * residual
                if k < REACH - 1:
                    later[w, :, lanes] = fresh
                if REACH <= w < REACH + 2:
                    totals[w - REACH] += jnp.where(k + 1 < limit, fresh, 0.0)
                before, here = here, after
            now, later = later, now
        for row in range(rows):
            change = totals[row] - gather(window, REACH + row, g, is_tail)
            if is_tail:
                change = jnp.concatenate(
                    [jnp.where(upper_half, change, 0.0), jnp.where(upper_half, 0.0, change)], axis=1)
            delta[row, part] = change

    few = jnp.concatenate([restore_sel[0], restore_sel[1], restore_sel[0]], axis=0)
    for row in range(rows):
        high, low = split(delta[row])
        out[row] += lax.dot_general(
            jnp.concatenate([high, high, low], axis=0), few, TN, preferred_element_type=f32)

    @pl.when(swift)
    def _():
        halo(0).wait_send()
        halo(chunks).wait_send()

    @pl.when(has_beyond)
    def _():
        for chunk in range(1, chunks):
            halo(chunk).wait_send()
            halo(chunk + chunks).wait_send()

    between.wait_send()

    @pl.when(is0)
    def _():
        for copy in lent:
            copy.wait_send()

    @pl.when(is1)
    def _():
        for tile in range(tiles):
            give(tile).wait_send()

    each(inner_sends, "wait_send")
    each(relays, "wait_send")
    each(outer_relays, "wait_send")
    for kind in kinds:
        for chunk in range(chunks):
            each(outer_sends(chunk, kind), "wait_send")


def solution(mesh):
    devices = mesh.shape["lat"]

    def local(state, east_wind, north_wind, coef, project, restore, stiffness, sweeps, mode_slots):
        rows, lons, levels = state.shape
        nlat = coef.shape[0]
        listed = mode_slots.shape[0] * mode_slots.shape[1] * 3 // 8
        full, rest = listed // 8, listed % 8
        tail = 1 if rest == 4 else 0
        full += 1 if rest and not tail else 0
        ranks = 8 * (full + tail)
        packed = full * lons + tail * lons // 2
        tiles = lons // 128
        copies = 9 + 14 * (tiles // 2)
        anywhere = pl.BlockSpec(memory_space=pl.ANY)
        vmem = pltpu.VMEM
        block = vmem((rows + 1, lons, levels), f32)
        return pl.pallas_call(
            functools.partial(kernel, devices, full, tail),
            out_shape=pltpu.VMEM(state.shape, f32),
            in_specs=[anywhere] * 9,
            out_specs=pl.BlockSpec(memory_space=pltpu.VMEM),
            scratch_shapes=[
                block, block, block,
                vmem(coef.shape, f32), vmem(project.shape, f32), vmem(restore.shape, f32),
                vmem((1, levels), f32), vmem((1, levels), jnp.int32),
                vmem(mode_slots.shape[::-1], jnp.int32),
                vmem((2, lons, levels), f32), vmem((lons, levels), f32), vmem((2, lons, levels), f32),
                vmem((lons, levels), f32),
                vmem((rows + 1, 8, packed), f32), vmem((WINDOW, 8, packed), f32),
                vmem((WINDOW, 8, packed), f32), vmem((WINDOW, 8, packed), f32),
                vmem((WINDOW, 8, packed), f32),
                vmem((rows, ranks, lons), f32), vmem((WINDOW - 2, 8, packed), f32),
                vmem((WINDOW - 2, 8, packed), f32), vmem((2 * REACH + 2, ranks, 128), f32),
                pltpu.SemaphoreType.DMA((9,)),
                pltpu.SemaphoreType.DMA((3 * tiles + 4,)), pltpu.SemaphoreType.DMA((3 * tiles + 4,)),
                pltpu.SemaphoreType.DMA((copies,)), pltpu.SemaphoreType.DMA((copies,)),
                pltpu.SemaphoreType.REGULAR((5,)),
            ],
            compiler_params=pltpu.CompilerParams(
                collective_id=0, has_side_effects=True, vmem_limit_bytes=VMEM_LIMIT),
        )(state, east_wind, north_wind, coef, project, restore, stiffness.reshape(1, levels),
          sweeps.reshape(1, levels), mode_slots.T)

    placed = (
        P(("parts", "lat"), None, None),
        P(("parts", "lat"), None, None),
        P(("parts", "lat"), None, None),
        P("parts", None),
        P(),
        P(),
        P(),
        P(),
        P("parts", None),
    )
    return jax.shard_map(
        local,
        mesh=mesh,
        in_specs=placed,
        out_specs=P(("parts", "lat"), None, None),
        check_vma=False,
    )
```
